32 devices in a mesh: groups: 2 (over x), pair: 16 (over z, y, core).
Axes of the slice: x: 2, y: 2, z: 4, core: 2. Of those that a mesh axis runs over, the one named last changes fastest.
Arguments:
- answer_states: bfloat16 [128, 128, 5120], P(('groups', 'pair')), parts along dimension 0, may hold values from -6 to 6
- prompt_states: bfloat16 [512, 8, 5120], P(('groups', 'pair')), parts along dimension 0, may hold values from -6 to 6
- queries: bfloat16 [512, 8, 4096], P(('groups', 'pair')), parts along dimension 0, may hold values from -6 to 6
- w_key: bfloat16 [5120, 512], P('pair'), may hold values from -0.078125 to 0.078125
- w_value: bfloat16 [5120, 512], P('pair'), may hold values from -0.078125 to 0.078125
- key_gain: float32 [128], replicated, may hold values from 0.5 to 2
- query_gain: float32 [128], replicated, may hold values from 0.5 to 2
- pair_list: int32 [512, 2], P('groups'), parts along dimension 0, may hold values from 0 to 63, as said below
- answer_row: int32 [128], P('groups'), parts along dimension 0, may hold values from 0 to 63, as said below
- lengths: int32 [128], P('groups'), parts along dimension 0, may hold values from 1 to 128, 2048 in all
Outputs:
- attended: bfloat16 [512, 8, 4096], P(('groups', 'pair')), parts along dimension 0
The draws below stay inside these ranges and needn't reach their ends.
There are 2 independent parts, one for each index of `groups`. The reference program is written for one: setup_inputs(seed, part) draws one part's arguments, and reference() takes and returns one part's arrays. A program takes and returns all parts, laid end to end along the dimension named above; an argument that names none is the same for every part. Nothing has to cross between parts.
Inputs may be any that keep to these rules, and one draw needn't show every extreme that they name: `pair_list`: the two ids of a row differ. Row r + 128 is row r reversed, for r < 128. The 32 ids in the rows of one device (aligned blocks of 16 rows) are distinct, and at most 2 of them have answer_row // 4 equal to one value; exactly 2 for some. `answer_row`: A permutation.
All inputs are finite; a program needn't handle non-finite values.
Results may differ from the reference program's by a relative error of at most 0.0086.
Values may be sent and summed in bfloat16 or wider, within the bound.
A program may use at most 128 MiB of HBM per device.

```python
import math
import jax
import jax.numpy as jnp
import numpy as np
from jax import lax

D = 5120
HQ = 32
HK = 4
HD = 128
ALEN = 128
PLEN = 8
ANS_DEV = 4
PAIRS_DEV = 16
ANSWERS = 64
PAIRS = 256


def shared_rows(key):
    return jax.random.permutation(key, ANSWERS).astype(jnp.int32)


def draw_answer_row(key, part):
    return shared_rows(key)


def owner_order(perm_key, owners_count):
    return jax.random.permutation(perm_key, owners_count).astype(jnp.int32)


def draw_pair_list(key, part):
    answer_row = shared_rows(key)
    inverse = jnp.argsort(answer_row, stable=True).astype(jnp.int32)
    key = jax.random.fold_in(key, 11)
    owners_count = ANSWERS // ANS_DEV
    halves = PAIRS // (2 * PAIRS_DEV)
    refs = 2 * PAIRS_DEV
    perm_keys = jax.random.split(jax.random.fold_in(key, 1), halves)
    owner_perm = jax.vmap(lambda perm_key: owner_order(perm_key, owners_count))(perm_keys)
    ref_index = jnp.arange(refs, dtype=jnp.int32)
    owners = owner_perm[:, ref_index % owners_count]
    offsets = jax.random.randint(jax.random.fold_in(key, 2), (halves, owners_count), 0, ANS_DEV).astype(jnp.int32)
    offset_of = jnp.take_along_axis(offsets, owners, axis=1)
    slots = (ref_index[None, :] // owners_count + offset_of) % ANS_DEV
    rows = owners * ANS_DEV + slots
    idents = inverse[rows]
    first = idents.reshape(halves, PAIRS_DEV, 2)
    second = first[:, :, ::-1]
    return jnp.concatenate([first, second], axis=0).reshape(PAIRS, 2).astype(jnp.int32)


def steps_of(own_key, extent, pieces, low, high):
    def one(axis_at, blocks):
        draws = jax.random.uniform(jax.random.fold_in(jax.random.fold_in(own_key, 6), axis_at), (blocks,), jnp.float32, low / len(pieces), high / len(pieces))
        return jnp.repeat(jnp.exp(draws), extent[axis_at] // blocks).reshape((-1,) + (1,) * (len(extent) - axis_at - 1))

    level = one(*pieces[0])
    for cut in pieces[1:]:
        level = level * one(*cut)
    return level


def split_up(count, total, reach, skew):
    loads = [(1 << 20) // math.isqrt(grade ** skew) + 1 for grade in range(2, count + 1)]
    spare, counts = total - reach - (count - 1), [1] * (count - 1)
    while spare > 0:
        movable = [i for i in range(count - 1) if counts[i] < reach]
        pool, left = sum([loads[i] for i in movable]), spare
        for i in movable:
            more = min(reach - counts[i], max(1, left * loads[i] // pool), spare)
            counts[i] = counts[i] + more
            spare = spare - more
    return np.array([reach] + counts)


def uneven(stream_key, number_of, total, reach, skew):
    if number_of == 2:
        one = jax.random.randint(stream_key, (), max(1, total - reach), min(reach, total - 1) + 1)
        return jnp.stack([one, total - one])
    tallies = jnp.asarray(split_up(number_of, total, reach, skew), jnp.int32)
    twos = (number_of - 1) // 2
    giver, receiver = tallies[1:1 + 2 * twos:2], tallies[2:2 + 2 * twos:2]
    margin = jnp.minimum(giver - 1, reach - receiver)
    passed = jax.random.randint(jax.random.fold_in(stream_key, 1), (twos,), 0, 1 << 20) % (margin + 1)
    tallies = tallies.at[1:1 + 2 * twos:2].set(giver - passed).at[2:2 + 2 * twos:2].set(receiver + passed)
    return tallies[jax.random.permutation(jax.random.fold_in(stream_key, 2), number_of)]


def normal_values(stream_key, dims, spread, reach, shards=(), held_as=jnp.bfloat16):
    factor_of = steps_of(stream_key, dims, shards, -0.22, 0.18) if shards else 1.0
    drawn = jax.random.normal(stream_key, dims, jnp.float32) * spread * factor_of
    return jnp.minimum(jnp.maximum(drawn, -reach), reach).astype(held_as)


def setup_inputs(seed: int = 0, part: int = 0) -> dict:
    key_of = jax.random.split(jax.random.key(seed), 11)
    part_splits = jax.random.split(jax.random.fold_in(key_of[10], part), 11)
    answer_states = normal_values(part_splits[0], (ANSWERS, ALEN, D), 1.0, 6.0, ((0, 16),))
    prompt_states = normal_values(part_splits[1], (PAIRS, PLEN, D), 1.0, 6.0, ((0, 16),))
    queries = normal_values(part_splits[2], (PAIRS, PLEN, HQ * HD), 1.0, 6.0, ((0, 16),))
    w_key = normal_values(key_of[3], (D, HK * HD), D ** -0.5, 0.078125, ((0, 16),))
    w_value = normal_values(key_of[4], (D, HK * HD), D ** -0.5, 0.078125, ((0, 16),))
    key_gain = jnp.clip(jnp.exp(jax.random.uniform(key_of[5], (HD,), jnp.float32, math.log(0.5), math.log(2.0))), 0.5, 2.0)
    query_gain = jnp.clip(jnp.exp(jax.random.uniform(key_of[6], (HD,), jnp.float32, math.log(0.5), math.log(2.0))), 0.5, 2.0)
    pair_list = draw_pair_list(jax.random.fold_in(jax.random.fold_in(key_of[10], part), 71), part)
    answer_row = draw_answer_row(jax.random.fold_in(jax.random.fold_in(key_of[10], part), 71), part)
    lengths = uneven(part_splits[9], ANSWERS, ANSWERS * ALEN // 4, ALEN, 1).astype(jnp.int32)
    return dict(answer_states=answer_states, prompt_states=prompt_states, queries=queries, w_key=w_key, w_value=w_value, key_gain=key_gain, query_gain=query_gain, pair_list=pair_list, answer_row=answer_row, lengths=lengths)


norm_eps = 1e-06

def head_norm(values_in, gain, heads):
    shaped = values_in.reshape(values_in.shape[:-1] + (heads, gain.shape[0]))
    scale = lax.rsqrt(lax.optimization_barrier(jnp.mean(shaped * shaped, axis=-1, keepdims=True)) + norm_eps)
    return (shaped * scale * gain).reshape(values_in.shape)

def group_partial(query_rows, key_rows, value_rows, valid):
    groups = HQ // HK
    query_four = query_rows.astype(jnp.float32).reshape(PLEN, HK, groups, HD)
    key_three = key_rows.astype(jnp.float32).reshape(key_rows.shape[0], HK, HD)
    value_three = value_rows.astype(jnp.float32).reshape(value_rows.shape[0], HK, HD)
    scores = jnp.einsum('qkgd,lkd->kgql', query_four, key_three) * HD ** (-0.5)
    weights = jnp.where(valid[None, None], jnp.exp(scores), jnp.float32(0.0))
    totals = lax.optimization_barrier(jnp.sum(weights, axis=-1))
    rounded = weights.astype(jnp.bfloat16).astype(jnp.float32)
    numer = jnp.einsum('kgql,lkd->qkgd', rounded, value_three)
    totals_q = jnp.transpose(totals, (2, 0, 1))
    mixed = (numer / totals_q[..., None]).astype(jnp.bfloat16)
    return (mixed.reshape(PLEN, HQ, HD), totals_q.reshape(PLEN, HQ))

def reference(answer_states, prompt_states, queries, w_key, w_value, key_gain, query_gain, pair_list, answer_row, lengths):

    def project(states):
        key_raw = jnp.dot(states, w_key, preferred_element_type=jnp.float32)
        keys_out = head_norm(key_raw, key_gain, HK).astype(jnp.bfloat16)
        values_out = jnp.dot(states, w_value, preferred_element_type=jnp.float32).astype(jnp.bfloat16)
        return (keys_out, values_out)
    answer_keys, answer_values = lax.map(project, answer_states)
    prompt_keys, prompt_values = lax.map(project, prompt_states)
    query_normed = head_norm(queries.astype(jnp.float32), query_gain, HQ).astype(jnp.bfloat16)
    positions = jnp.arange(ALEN, dtype=jnp.int32)
    causal = jnp.arange(PLEN)[:, None] >= jnp.arange(PLEN)[None, :]

    def one_pair(inputs):
        query_rows, own_keys, own_values, pair_ids = inputs
        results = [group_partial(query_rows, own_keys, own_values, causal)]
        for side in range(2):
            ident = pair_ids[side]
            row = answer_row[ident]
            valid = jnp.broadcast_to(positions[None, :] < lengths[ident], (PLEN, ALEN))
            results.append(group_partial(query_rows, answer_keys[row], answer_values[row], valid))
        numer = jnp.zeros((PLEN, HQ, HD), jnp.float32)
        denom = jnp.zeros((PLEN, HQ), jnp.float32)
        for mixed, totals in results:
            numer = numer + totals[..., None] * mixed.astype(jnp.float32)
            denom = denom + totals
        return (numer / denom[..., None]).reshape(PLEN, HQ * HD).astype(jnp.bfloat16)
    return lax.map(one_pair, (query_normed, prompt_keys, prompt_values, pair_list))
```

```python
import functools
import jax
import jax.numpy as jnp
from jax import lax
from jax.experimental import pallas as pl
from jax.experimental.pallas import tpu as pltpu
from jax.sharding import PartitionSpec as P

norm_eps = 1e-06
VMEM = pltpu.VMEM
LIMIT = 48 * 1024 * 1024
USE_RING = False


def table_lookup(table, indices):
    match = indices[..., None] == jnp.arange(table.shape[0], dtype=jnp.int32)
    return jnp.sum(jnp.where(match, table, 0), axis=-1)


def earlier_same(owners):
    width_refs = owners.shape[-1]
    earlier = jnp.arange(width_refs)[:, None] > jnp.arange(width_refs)[None, :]
    same = owners[..., :, None] == owners[..., None, :]
    return jnp.sum(same & earlier, axis=-1)


def norm_rows(x, gain):
    scale = lax.rsqrt(jnp.mean(x * x, axis=-1, keepdims=True) + norm_eps)
    return x * scale * gain


def query_kernel(pairs, plen, heads, hd, slots, idx_ref, q_ref, gain_ref, own_ref, out_ref):
    gain = gain_ref[...]
    for two in range(heads // 2):
        parts = [
            norm_rows(q_ref[:, (2 * two + e) * hd : (2 * two + e + 1) * hd].astype(jnp.float32), gain)
            for e in range(2)
        ]
        for p in range(pairs):
            rows = jnp.concatenate([x[p * plen : (p + 1) * plen] for x in parts], axis=0)
            own_ref[p, two * 2 * plen : (two + 1) * 2 * plen, :] = rows.astype(jnp.bfloat16)

    def body(s, carry):
        out_ref[s] = own_ref[idx_ref[s]]
        return carry

    lax.fori_loop(0, slots, body, 0)


def prepare_queries(idx, queries, gain):
    pairs, plen, width = queries.shape
    hd = gain.shape[0]
    heads = width // hd
    slots = idx.shape[0]
    return pl.pallas_call(
        functools.partial(query_kernel, pairs, plen, heads, hd, slots),
        out_shape=[
            jax.ShapeDtypeStruct((pairs, heads * plen, hd), jnp.bfloat16),
            jax.ShapeDtypeStruct((slots, heads * plen, hd), jnp.bfloat16),
        ],
        in_specs=[
            pl.BlockSpec(memory_space=pltpu.SMEM),
            pl.BlockSpec(memory_space=VMEM),
            pl.BlockSpec(memory_space=VMEM),
        ],
        out_specs=[pl.BlockSpec(memory_space=VMEM)] * 2,
        compiler_params=pltpu.CompilerParams(vmem_limit_bytes=LIMIT),
    )(idx, queries.reshape(pairs * plen, width), gain.reshape(1, hd))


def project_kernel(hd, x_ref, wk_ref, wv_ref, gain_ref, k_ref, v_ref):
    x = x_ref[...]
    raw = jnp.dot(x, wk_ref[...], preferred_element_type=jnp.float32)
    for h in range(raw.shape[1] // hd):
        cols = slice(h * hd, (h + 1) * hd)
        k_ref[:, cols] = norm_rows(raw[:, cols], gain_ref[...]).astype(jnp.bfloat16)
    v_ref[...] = jnp.dot(x, wv_ref[...], preferred_element_type=jnp.float32).astype(jnp.bfloat16)


def project(x, wk, wv, gain):
    rows, width = x.shape
    kvw = wk.shape[1]
    hd = gain.shape[0]
    block = 128
    whole = pl.BlockSpec((width, kvw), lambda i: (0, 0), pipeline_mode=pl.Buffered(1))
    return pl.pallas_call(
        functools.partial(project_kernel, hd),
        grid=(rows // block,),
        out_shape=[jax.ShapeDtypeStruct((rows, kvw), jnp.bfloat16)] * 2,
        in_specs=[
            pl.BlockSpec((block, width), lambda i: (i, 0)),
            whole,
            whole,
            pl.BlockSpec((1, hd), lambda i: (0, 0)),
        ],
        out_specs=[pl.BlockSpec((block, kvw), lambda i: (i, 0))] * 2,
        compiler_params=pltpu.CompilerParams(vmem_limit_bytes=LIMIT),
    )(x, wk, wv, gain.reshape(1, hd))


def attend(q, k, v, valid, scale):
    scores = lax.dot_general(q, k, (((1,), (1,)), ((), ())), preferred_element_type=jnp.float32) * scale
    weights = jnp.where(valid, jnp.exp(scores), 0.0)
    total = jnp.sum(weights, axis=-1, keepdims=True)
    numer = jnp.dot(weights.astype(jnp.bfloat16), v, preferred_element_type=jnp.float32)
    return (numer / total).astype(jnp.bfloat16), total


def owner_kernel(per, kvh, hd, scale, slot_ref, len_ref, q_ref, k_ref, v_ref, o_ref, t_ref):
    step = pl.program_id(0)
    rows = q_ref.shape[1]
    each = rows // kvh
    for e in range(per):
        ref = step * per + e
        row = slot_ref[ref]
        count = len_ref[ref]
        totals = []
        for h in range(kvh):
            cols = slice(h * hd, (h + 1) * hd)
            keys = k_ref[row, :, cols]
            position = lax.broadcasted_iota(jnp.int32, (each, keys.shape[0]), 1)
            mixed, total = attend(
                q_ref[e, h * each : (h + 1) * each, :], keys, v_ref[row, :, cols], position < count, scale
            )
            o_ref[e, h * each : (h + 1) * each, :] = mixed
            totals.append(jnp.broadcast_to(total, (each, hd)))
        t_ref[e] = jnp.concatenate(totals, axis=0).T[:8]


def owner_attention(slot, lens, q, keys, values, hd):
    slots, rows, _ = q.shape
    _, alen, kvw = keys.shape
    per = 4
    spec = lambda shape, f: pl.BlockSpec(shape, f)
    return pl.pallas_call(
        functools.partial(owner_kernel, per, kvw // hd, hd, hd ** (-0.5)),
        grid_spec=pltpu.PrefetchScalarGridSpec(
            num_scalar_prefetch=2,
            grid=(slots // per,),
            in_specs=[
                spec((per, rows, hd), lambda i, *_: (i, 0, 0)),
                spec(keys.shape, lambda i, *_: (0, 0, 0)),
                spec(keys.shape, lambda i, *_: (0, 0, 0)),
            ],
            out_specs=[
                spec((per, rows, hd), lambda i, *_: (i, 0, 0)),
                spec((per, 8, rows), lambda i, *_: (i, 0, 0)),
            ],
        ),
        out_shape=[
            jax.ShapeDtypeStruct((slots, rows, hd), jnp.bfloat16),
            jax.ShapeDtypeStruct((slots, 8, rows), jnp.float32),
        ],
        compiler_params=pltpu.CompilerParams(vmem_limit_bytes=LIMIT),
    )(slot, lens, q, keys, values)


def combine_kernel(per, plen, kvh, hd, scale, at_ref, q_ref, k_ref, v_ref, in_ref, t_ref, o_ref):
    step = pl.program_id(0)
    rows = q_ref.shape[1]
    each = rows // kvh
    keys_count = k_ref.shape[0]
    results = []
    for e in range(per):
        pair = step * per + e
        place = lax.broadcasted_iota(jnp.int32, (each, keys_count), 1)
        token = lax.broadcasted_iota(jnp.int32, (each, keys_count), 0) % plen
        valid = (place // plen == pair) & (place % plen <= token)
        numers, denoms = [], []
        for h in range(kvh):
            cols = slice(h * hd, (h + 1) * hd)
            mixed, total = attend(
                q_ref[e, h * each : (h + 1) * each, :], k_ref[:, cols], v_ref[:, cols], valid, scale
            )
            numers.append(total * mixed.astype(jnp.float32))
            denoms.append(jnp.broadcast_to(total, (each, hd)))
        numer = jnp.concatenate(numers, axis=0)
        denom = jnp.concatenate(denoms, axis=0)
        for side in range(2):
            at = at_ref[pair * 2 + side]
            total = jnp.broadcast_to(t_ref[at][:1], (hd, rows)).T
            numer = numer + total * in_ref[at].astype(jnp.float32)
            denom = denom + total
        results.append(numer / denom)
    for head in range(rows // plen):
        block = jnp.concatenate([r[head * plen : (head + 1) * plen] for r in results], axis=0)
        o_ref[:, head * hd : (head + 1) * hd] = block.astype(jnp.bfloat16)


def combine(at, q, keys, values, incoming, totals, plen, hd):
    pairs, rows, _ = q.shape
    slots = incoming.shape[0]
    kvw = keys.shape[1]
    per = 4
    heads = rows // plen
    return pl.pallas_call(
        functools.partial(combine_kernel, per, plen, kvw // hd, hd, hd ** (-0.5)),
        grid_spec=pltpu.PrefetchScalarGridSpec(
            num_scalar_prefetch=1,
            grid=(pairs // per,),
            in_specs=[
                pl.BlockSpec((per, rows, hd), lambda i, *_: (i, 0, 0)),
                pl.BlockSpec(keys.shape, lambda i, *_: (0, 0)),
                pl.BlockSpec(keys.shape, lambda i, *_: (0, 0)),
                pl.BlockSpec(incoming.shape, lambda i, *_: (0, 0, 0)),
                pl.BlockSpec(totals.shape, lambda i, *_: (0, 0, 0)),
            ],
            out_specs=pl.BlockSpec((per * plen, heads * hd), lambda i, *_: (i, 0)),
        ),
        out_shape=jax.ShapeDtypeStruct((pairs * plen, heads * hd), jnp.bfloat16),
        compiler_params=pltpu.CompilerParams(vmem_limit_bytes=LIMIT),
    )(at, q, keys, values, incoming, totals)


def ring_kernel(chips, wk_ref, wv_ref, ok_ref, ov_ref, own_sem, ring_send, ring_recv, side_send, side_recv):
    me = lax.axis_index("pair")
    group = lax.axis_index("groups")
    depth = wk_ref.shape[0]
    chip, core = me // 2, me % 2
    even = chip % 2
    position = jnp.where(even == 0, chip // 2, chips - 1 - chip // 2)

    def chip_at(place):
        place = (place + 2 * chips) % chips
        return jnp.where(place < chips // 2, 2 * place, 2 * (chips - 1 - place) + 1)

    right = chip_at(position + 1) * 2 + core
    left = chip_at(position - 1) * 2 + core
    sibling = chip * 2 + 1 - core
    partners = (right, left)
    mesh_id = pl.DeviceIdType.MESH

    barrier = pltpu.get_barrier_semaphore()
    for other in (right, left, sibling):
        pl.semaphore_signal(barrier, inc=1, device_id=(group, other), device_id_type=mesh_id)
    own = []
    outs = (ok_ref, ov_ref)
    for w, (src, out) in enumerate(((wk_ref, ok_ref), (wv_ref, ov_ref))):
        copy = pltpu.make_async_copy(src, out.at[me], own_sem.at[w])
        copy.start()
        own.append(copy)
    for copy in own:
        copy.wait()
    pl.semaphore_wait(barrier, 3)

    def piece(w, step):
        return chip_at(position - step if w == 0 else position + step) * 2 + core

    def ring(w, step):
        block = outs[w].at[piece(w, step)]
        return pltpu.make_async_remote_copy(
            src_ref=block, dst_ref=block, send_sem=ring_send.at[w, step], recv_sem=ring_recv.at[w, step],
            device_id=(group, partners[w]), device_id_type=mesh_id,
        )

    def arriving(w, step):
        block = outs[w].at[piece(w, step + 1)]
        return pltpu.make_async_remote_copy(
            src_ref=block, dst_ref=block, send_sem=ring_send.at[w, step], recv_sem=ring_recv.at[w, step],
            device_id=(group, partners[w]), device_id_type=mesh_id,
        )

    def across(w, step, mine):
        block = outs[w].at[piece(w, step) if mine else chip_at(position - step if w == 0 else position + step) * 2 + 1 - core]
        return pltpu.make_async_remote_copy(
            src_ref=block, dst_ref=block, send_sem=side_send.at[w, step], recv_sem=side_recv.at[w, step],
            device_id=(group, sibling), device_id_type=mesh_id,
        )

    for w in range(2):
        ring(w, 0).start()
        across(w, 0, True).start()

    def body(step, carry):
        for w in range(2):
            arriving(w, step - 1).wait_recv()

            @pl.when(step < chips - 1)
            def _():
                ring(w, step).start()

            across(w, step, True).start()
        return carry

    lax.fori_loop(1, chips, body, 0)

    def drain(step, carry):
        for w in range(2):
            across(w, step, True).wait_send()
            across(w, step, False).wait_recv()

            @pl.when(step < chips - 1)
            def _():
                ring(w, step).wait_send()

        return carry

    lax.fori_loop(0, chips, drain, 0)


def gather_weights(w_key, w_value):
    peers = lax.axis_size("pair")
    depth, kvw = w_key.shape
    if not USE_RING:
        return tuple(lax.all_gather(w, "pair", axis=0, tiled=True) for w in (w_key, w_value))
    chips = peers // 2
    hbm = pl.BlockSpec(memory_space=pl.ANY)
    out = pl.pallas_call(
        functools.partial(ring_kernel, chips),
        out_shape=[jax.ShapeDtypeStruct((peers, depth, kvw), jnp.bfloat16)] * 2,
        in_specs=[hbm] * 2,
        out_specs=[hbm] * 2,
        scratch_shapes=[pltpu.SemaphoreType.DMA((2,))] + [pltpu.SemaphoreType.DMA((2, chips))] * 4,
        compiler_params=pltpu.CompilerParams(
            collective_id=0, has_side_effects=True, vmem_limit_bytes=LIMIT
        ),
    )(w_key, w_value)
    return tuple(w.reshape(peers * depth, kvw) for w in out)


def per_device(
    answer_states, prompt_states, queries, w_key, w_value, key_gain, query_gain, pair_list, answer_row, lengths
):
    device = lax.axis_index("pair")
    peers = lax.axis_size("pair")
    ans_dev, ans_len, width = answer_states.shape
    pairs_dev, prompt_len = (queries.shape[0], queries.shape[1])
    head_dim = key_gain.shape[0]
    kv_width = w_key.shape[1]
    refs = 2 * pairs_dev
    capacity = (refs + peers - 1) // peers
    slots = peers * capacity

    all_ids = pair_list.reshape(peers, refs)
    all_rows = table_lookup(answer_row, all_ids)
    all_owner = all_rows // ans_dev
    all_local = all_rows % ans_dev
    all_rank = earlier_same(all_owner)
    all_lens = table_lookup(lengths, all_ids)
    my_owner = lax.dynamic_index_in_dim(all_owner, device, 0, keepdims=False)
    my_rank = lax.dynamic_index_in_dim(all_rank, device, 0, keepdims=False)
    fetch_index = my_owner * capacity + my_rank
    slot_ids = jnp.arange(slots, dtype=jnp.int32)
    ref_match = fetch_index[None, :] == slot_ids[:, None]
    ref_pair = jnp.sum(jnp.where(ref_match, jnp.arange(refs, dtype=jnp.int32)[None, :] // 2, 0), axis=1)
    slot_range = jnp.arange(capacity, dtype=jnp.int32)
    slot_match = (all_owner == device)[:, None, :] & (all_rank[:, None, :] == slot_range[None, :, None])
    slot_local = jnp.sum(jnp.where(slot_match, all_local[:, None, :], 0), axis=-1).reshape(slots)
    slot_lens = jnp.sum(jnp.where(slot_match, all_lens[:, None, :], 0), axis=-1).reshape(slots)
    slot_lens = jnp.maximum(slot_lens, 1)

    query_own, outgoing = prepare_queries(ref_pair, queries, query_gain)
    asked = lax.all_to_all(outgoing, "pair", split_axis=0, concat_axis=0, tiled=True)
    key_full, value_full = gather_weights(w_key, w_value)
    answer_keys, answer_values = project(
        answer_states.reshape(ans_dev * ans_len, width), key_full, value_full, key_gain
    )
    mixed, totals = owner_attention(
        slot_local,
        slot_lens,
        asked,
        answer_keys.reshape(ans_dev, ans_len, kv_width),
        answer_values.reshape(ans_dev, ans_len, kv_width),
        head_dim,
    )
    mixed_in = lax.all_to_all(mixed, "pair", split_axis=0, concat_axis=0, tiled=True)
    totals_in = lax.all_to_all(totals, "pair", split_axis=0, concat_axis=0, tiled=True)
    prompt_keys, prompt_values = project(
        prompt_states.reshape(pairs_dev * prompt_len, width), key_full, value_full, key_gain
    )
    out = combine(
        fetch_index, query_own, prompt_keys, prompt_values, mixed_in, totals_in, prompt_len, head_dim
    )
    return out.reshape(queries.shape)


def solution(mesh):
    in_specs = (
        P(("groups", "pair"), None, None),
        P(("groups", "pair"), None, None),
        P(("groups", "pair"), None, None),
        P("pair", None),
        P("pair", None),
        P(),
        P(),
        P("groups", None),
        P("groups"),
        P("groups"),
    )
    out_specs = P(("groups", "pair"), None, None)
    return jax.shard_map(
        per_device, mesh=mesh, in_specs=in_specs, out_specs=out_specs, check_vma=False
    )
```

```python
import functools
import jax
import jax.numpy as jnp
from jax import lax
from jax.experimental import pallas as pl
from jax.experimental.pallas import tpu as pltpu
from jax.sharding import PartitionSpec as P

norm_eps = 1e-06
VMEM = pltpu.VMEM
LIMIT = 48 * 1024 * 1024
USE_RING = True


def table_lookup(table, indices):
    match = indices[..., None] == jnp.arange(table.shape[0], dtype=jnp.int32)
    return jnp.sum(jnp.where(match, table, 0), axis=-1)


def earlier_same(owners):
    width_refs = owners.shape[-1]
    earlier = jnp.arange(width_refs)[:, None] > jnp.arange(width_refs)[None, :]
    same = owners[..., :, None] == owners[..., None, :]
    return jnp.sum(same & earlier, axis=-1)


def norm_rows(x, gain):
    scale = lax.rsqrt(jnp.mean(x * x, axis=-1, keepdims=True) + norm_eps)
    return x * scale * gain


def query_kernel(pairs, plen, heads, hd, slots, idx_ref, q_ref, gain_ref, own_ref, out_ref):
    gain = gain_ref[...]
    for two in range(heads // 2):
        parts = [
            norm_rows(q_ref[:, (2 * two + e) * hd : (2 * two + e + 1) * hd].astype(jnp.float32), gain)
            for e in range(2)
        ]
        for p in range(pairs):
            rows = jnp.concatenate([x[p * plen : (p + 1) * plen] for x in parts], axis=0)
            own_ref[p, two * 2 * plen : (two + 1) * 2 * plen, :] = rows.astype(jnp.bfloat16)

    def body(s, carry):
        out_ref[s] = own_ref[idx_ref[s]]
        return carry

    lax.fori_loop(0, slots, body, 0)


def prepare_queries(idx, queries, gain):
    pairs, plen, width = queries.shape
    hd = gain.shape[0]
    heads = width // hd
    slots = idx.shape[0]
    return pl.pallas_call(
        functools.partial(query_kernel, pairs, plen, heads, hd, slots),
        out_shape=[
            jax.ShapeDtypeStruct((pairs, heads * plen, hd), jnp.bfloat16),
            jax.ShapeDtypeStruct((slots, heads * plen, hd), jnp.bfloat16),
        ],
        in_specs=[
            pl.BlockSpec(memory_space=pltpu.SMEM),
            pl.BlockSpec(memory_space=VMEM),
            pl.BlockSpec(memory_space=VMEM),
        ],
        out_specs=[pl.BlockSpec(memory_space=VMEM)] * 2,
        compiler_params=pltpu.CompilerParams(vmem_limit_bytes=LIMIT),
    )(idx, queries.reshape(pairs * plen, width), gain.reshape(1, hd))


def project_kernel(hd, x_ref, wk_ref, wv_ref, gain_ref, k_ref, v_ref):
    x = x_ref[...]
    raw = jnp.dot(x, wk_ref[...], preferred_element_type=jnp.float32)
    for h in range(raw.shape[1] // hd):
        cols = slice(h * hd, (h + 1) * hd)
        k_ref[:, cols] = norm_rows(raw[:, cols], gain_ref[...]).astype(jnp.bfloat16)
    v_ref[...] = jnp.dot(x, wv_ref[...], preferred_element_type=jnp.float32).astype(jnp.bfloat16)


def project(x, wk, wv, gain):
    rows, width = x.shape
    kvw = wk.shape[1]
    hd = gain.shape[0]
    block = 128
    whole = pl.BlockSpec((width, kvw), lambda i: (0, 0), pipeline_mode=pl.Buffered(1))
    return pl.pallas_call(
        functools.partial(project_kernel, hd),
        grid=(rows // block,),
        out_shape=[jax.ShapeDtypeStruct((rows, kvw), jnp.bfloat16)] * 2,
        in_specs=[
            pl.BlockSpec((block, width), lambda i: (i, 0)),
            whole,
            whole,
            pl.BlockSpec((1, hd), lambda i: (0, 0)),
        ],
        out_specs=[pl.BlockSpec((block, kvw), lambda i: (i, 0))] * 2,
        compiler_params=pltpu.CompilerParams(vmem_limit_bytes=LIMIT),
    )(x, wk, wv, gain.reshape(1, hd))


def attend(q, k, v, valid, scale):
    scores = lax.dot_general(q, k, (((1,), (1,)), ((), ())), preferred_element_type=jnp.float32) * scale
    weights = jnp.where(valid, jnp.exp(scores), 0.0)
    total = jnp.sum(weights, axis=-1, keepdims=True)
    numer = jnp.dot(weights.astype(jnp.bfloat16), v, preferred_element_type=jnp.float32)
    return (numer / total).astype(jnp.bfloat16), total


def owner_kernel(per, kvh, hd, scale, slot_ref, len_ref, q_ref, k_ref, v_ref, o_ref, t_ref):
    step = pl.program_id(0)
    rows = q_ref.shape[1]
    each = rows // kvh
    for e in range(per):
        ref = step * per + e
        row = slot_ref[ref]
        count = len_ref[ref]
        totals = []
        for h in range(kvh):
            cols = slice(h * hd, (h + 1) * hd)
            keys = k_ref[row, :, cols]
            position = lax.broadcasted_iota(jnp.int32, (each, keys.shape[0]), 1)
            mixed, total = attend(
                q_ref[e, h * each : (h + 1) * each, :], keys, v_ref[row, :, cols], position < count, scale
            )
            o_ref[e, h * each : (h + 1) * each, :] = mixed
            totals.append(jnp.broadcast_to(total, (each, hd)))
        t_ref[e] = jnp.concatenate(totals, axis=0).T[:8]


def owner_attention(slot, lens, q, keys, values, hd):
    slots, rows, _ = q.shape
    _, alen, kvw = keys.shape
    per = 4
    spec = lambda shape, f: pl.BlockSpec(shape, f)
    return pl.pallas_call(
        functools.partial(owner_kernel, per, kvw // hd, hd, hd ** (-0.5)),
        grid_spec=pltpu.PrefetchScalarGridSpec(
            num_scalar_prefetch=2,
            grid=(slots // per,),
            in_specs=[
                spec((per, rows, hd), lambda i, *_: (i, 0, 0)),
                spec(keys.shape, lambda i, *_: (0, 0, 0)),
                spec(keys.shape, lambda i, *_: (0, 0, 0)),
            ],
            out_specs=[
                spec((per, rows, hd), lambda i, *_: (i, 0, 0)),
                spec((per, 8, rows), lambda i, *_: (i, 0, 0)),
            ],
        ),
        out_shape=[
            jax.ShapeDtypeStruct((slots, rows, hd), jnp.bfloat16),
            jax.ShapeDtypeStruct((slots, 8, rows), jnp.float32),
        ],
        compiler_params=pltpu.CompilerParams(vmem_limit_bytes=LIMIT),
    )(slot, lens, q, keys, values)


def combine_kernel(per, plen, kvh, hd, scale, at_ref, q_ref, k_ref, v_ref, in_ref, t_ref, o_ref):
    step = pl.program_id(0)
    rows = q_ref.shape[1]
    each = rows // kvh
    keys_count = k_ref.shape[0]
    results = []
    for e in range(per):
        pair = step * per + e
        place = lax.broadcasted_iota(jnp.int32, (each, keys_count), 1)
        token = lax.broadcasted_iota(jnp.int32, (each, keys_count), 0) % plen
        valid = (place // plen == pair) & (place % plen <= token)
        numers, denoms = [], []
        for h in range(kvh):
            cols = slice(h * hd, (h + 1) * hd)
            mixed, total = attend(
                q_ref[e, h * each : (h + 1) * each, :], k_ref[:, cols], v_ref[:, cols], valid, scale
            )
            numers.append(total * mixed.astype(jnp.float32))
            denoms.append(jnp.broadcast_to(total, (each, hd)))
        numer = jnp.concatenate(numers, axis=0)
        denom = jnp.concatenate(denoms, axis=0)
        for side in range(2):
            at = at_ref[pair * 2 + side]
            total = jnp.broadcast_to(t_ref[at][:1], (hd, rows)).T
            numer = numer + total * in_ref[at].astype(jnp.float32)
            denom = denom + total
        results.append(numer / denom)
    for head in range(rows // plen):
        block = jnp.concatenate([r[head * plen : (head + 1) * plen] for r in results], axis=0)
        o_ref[:, head * hd : (head + 1) * hd] = block.astype(jnp.bfloat16)


def combine(at, q, keys, values, incoming, totals, plen, hd):
    pairs, rows, _ = q.shape
    slots = incoming.shape[0]
    kvw = keys.shape[1]
    per = 4
    heads = rows // plen
    return pl.pallas_call(
        functools.partial(combine_kernel, per, plen, kvw // hd, hd, hd ** (-0.5)),
        grid_spec=pltpu.PrefetchScalarGridSpec(
            num_scalar_prefetch=1,
            grid=(pairs // per,),
            in_specs=[
                pl.BlockSpec((per, rows, hd), lambda i, *_: (i, 0, 0)),
                pl.BlockSpec(keys.shape, lambda i, *_: (0, 0)),
                pl.BlockSpec(keys.shape, lambda i, *_: (0, 0)),
                pl.BlockSpec(incoming.shape, lambda i, *_: (0, 0, 0)),
                pl.BlockSpec(totals.shape, lambda i, *_: (0, 0, 0)),
            ],
            out_specs=pl.BlockSpec((per * plen, heads * hd), lambda i, *_: (i, 0)),
        ),
        out_shape=jax.ShapeDtypeStruct((pairs * plen, heads * hd), jnp.bfloat16),
        compiler_params=pltpu.CompilerParams(vmem_limit_bytes=LIMIT),
    )(at, q, keys, values, incoming, totals)


def ring_kernel(chips, wk_ref, wv_ref, ok_ref, ov_ref, own_sem, ring_send, ring_recv, side_send, side_recv):
    me = lax.axis_index("pair")
    group = lax.axis_index("groups")
    depth = wk_ref.shape[0]
    chip, core = me // 2, me % 2
    even = chip % 2
    position = (1 - even) * (chip // 2) + even * (chips - 1 - chip // 2)

    def chip_at(place):
        place = (place + 2 * chips) % chips
        back = place // (chips // 2)
        return (1 - back) * 2 * place + back * (2 * (chips - 1 - place) + 1)

    right = chip_at(position + 1) * 2 + core
    left = chip_at(position - 1) * 2 + core
    sibling = chip * 2 + 1 - core
    partners = (right, left)
    mesh_id = pl.DeviceIdType.MESH

    barrier = pltpu.get_barrier_semaphore()
    for other in (right, left, sibling):
        pl.semaphore_signal(barrier, inc=1, device_id=(group, other), device_id_type=mesh_id)
    own = []
    outs = (ok_ref, ov_ref)
    for w, (src, out) in enumerate(((wk_ref, ok_ref), (wv_ref, ov_ref))):
        copy = pltpu.make_async_copy(src, out.at[me], own_sem.at[w])
        copy.start()
        own.append(copy)
    for copy in own:
        copy.wait()
    pl.semaphore_wait(barrier, 3)

    def piece(w, step):
        return chip_at(position - step if w == 0 else position + step) * 2 + core

    def ring(w, step):
        block = outs[w].at[piece(w, step)]
        return pltpu.make_async_remote_copy(
            src_ref=block, dst_ref=block, send_sem=ring_send.at[w, step], recv_sem=ring_recv.at[w, step],
            device_id=(group, partners[w]), device_id_type=mesh_id,
        )

    def arriving(w, step):
        block = outs[w].at[piece(w, step + 1)]
        return pltpu.make_async_remote_copy(
            src_ref=block, dst_ref=block, send_sem=ring_send.at[w, step], recv_sem=ring_recv.at[w, step],
            device_id=(group, partners[w]), device_id_type=mesh_id,
        )

    def across(w, step, mine):
        block = outs[w].at[piece(w, step) if mine else chip_at(position - step if w == 0 else position + step) * 2 + 1 - core]
        return pltpu.make_async_remote_copy(
            src_ref=block, dst_ref=block, send_sem=side_send.at[w, step], recv_sem=side_recv.at[w, step],
            device_id=(group, sibling), device_id_type=mesh_id,
        )

    for w in range(2):
        ring(w, 0).start()
        across(w, 0, True).start()

    def body(step, carry):
        for w in range(2):
            arriving(w, step - 1).wait_recv()

            @pl.when(step < chips - 1)
            def _():
                ring(w, step).start()

            across(w, step, True).start()
        return carry

    lax.fori_loop(1, chips, body, 0)

    def drain(step, carry):
        for w in range(2):
            across(w, step, True).wait_send()
            across(w, step, False).wait_recv()

            @pl.when(step < chips - 1)
            def _():
                ring(w, step).wait_send()

        return carry

    lax.fori_loop(0, chips, drain, 0)


def gather_weights(w_key, w_value):
    peers = lax.axis_size("pair")
    depth, kvw = w_key.shape
    if not USE_RING:
        return tuple(lax.all_gather(w, "pair", axis=0, tiled=True) for w in (w_key, w_value))
    chips = peers // 2
    hbm = pl.BlockSpec(memory_space=pl.ANY)
    out = pl.pallas_call(
        functools.partial(ring_kernel, chips),
        out_shape=[jax.ShapeDtypeStruct((peers, depth, kvw), jnp.bfloat16)] * 2,
        in_specs=[hbm] * 2,
        out_specs=[hbm] * 2,
        scratch_shapes=[pltpu.SemaphoreType.DMA((2,))] + [pltpu.SemaphoreType.DMA((2, chips))] * 4,
        compiler_params=pltpu.CompilerParams(
            collective_id=0, has_side_effects=True, vmem_limit_bytes=LIMIT
        ),
    )(w_key, w_value)
    return tuple(w.reshape(peers * depth, kvw) for w in out)


def per_device(
    answer_states, prompt_states, queries, w_key, w_value, key_gain, query_gain, pair_list, answer_row, lengths
):
    device = lax.axis_index("pair")
    peers = lax.axis_size("pair")
    ans_dev, ans_len, width = answer_states.shape
    pairs_dev, prompt_len = (queries.shape[0], queries.shape[1])
    head_dim = key_gain.shape[0]
    kv_width = w_key.shape[1]
    refs = 2 * pairs_dev
    capacity = (refs + peers - 1) // peers
    slots = peers * capacity

    all_ids = pair_list.reshape(peers, refs)
    all_rows = table_lookup(answer_row, all_ids)
    all_owner = all_rows // ans_dev
    all_local = all_rows % ans_dev
    all_rank = earlier_same(all_owner)
    all_lens = table_lookup(lengths, all_ids)
    my_owner = lax.dynamic_index_in_dim(all_owner, device, 0, keepdims=False)
    my_rank = lax.dynamic_index_in_dim(all_rank, device, 0, keepdims=False)
    fetch_index = my_owner * capacity + my_rank
    slot_ids = jnp.arange(slots, dtype=jnp.int32)
    ref_match = fetch_index[None, :] == slot_ids[:, None]
    ref_pair = jnp.sum(jnp.where(ref_match, jnp.arange(refs, dtype=jnp.int32)[None, :] // 2, 0), axis=1)
    slot_range = jnp.arange(capacity, dtype=jnp.int32)
    slot_match = (all_owner == device)[:, None, :] & (all_rank[:, None, :] == slot_range[None, :, None])
    slot_local = jnp.sum(jnp.where(slot_match, all_local[:, None, :], 0), axis=-1).reshape(slots)
    slot_lens = jnp.sum(jnp.where(slot_match, all_lens[:, None, :], 0), axis=-1).reshape(slots)
    slot_lens = jnp.maximum(slot_lens, 1)

    query_own, outgoing = prepare_queries(ref_pair, queries, query_gain)
    asked = lax.all_to_all(outgoing, "pair", split_axis=0, concat_axis=0, tiled=True)
    key_full, value_full = gather_weights(w_key, w_value)
    answer_keys, answer_values = project(
        answer_states.reshape(ans_dev * ans_len, width), key_full, value_full, key_gain
    )
    mixed, totals = owner_attention(
        slot_local,
        slot_lens,
        asked,
        answer_keys.reshape(ans_dev, ans_len, kv_width),
        answer_values.reshape(ans_dev, ans_len, kv_width),
        head_dim,
    )
    mixed_in = lax.all_to_all(mixed, "pair", split_axis=0, concat_axis=0, tiled=True)
    totals_in = lax.all_to_all(totals, "pair", split_axis=0, concat_axis=0, tiled=True)
    prompt_keys, prompt_values = project(
        prompt_states.reshape(pairs_dev * prompt_len, width), key_full, value_full, key_gain
    )
    out = combine(
        fetch_index, query_own, prompt_keys, prompt_values, mixed_in, totals_in, prompt_len, head_dim
    )
    return out.reshape(queries.shape)


def solution(mesh):
    in_specs = (
        P(("groups", "pair"), None, None),
        P(("groups", "pair"), None, None),
        P(("groups", "pair"), None, None),
        P("pair", None),
        P("pair", None),
        P(),
        P(),
        P("groups", None),
        P("groups"),
        P("groups"),
    )
    out_specs = P(("groups", "pair"), None, None)
    return jax.shard_map(
        per_device, mesh=mesh, in_specs=in_specs, out_specs=out_specs, check_vma=False
    )
```

```python
import functools
import jax
import jax.numpy as jnp
from jax import lax
from jax.experimental import pallas as pl
from jax.experimental.pallas import tpu as pltpu
from jax.sharding import PartitionSpec as P

norm_eps = 1e-06
VMEM = pltpu.VMEM
LIMIT = 48 * 1024 * 1024
USE_RING = True


def table_lookup(table, indices):
    match = indices[..., None] == jnp.arange(table.shape[0], dtype=jnp.int32)
    return jnp.sum(jnp.where(match, table, 0), axis=-1)


def earlier_same(owners):
    width_refs = owners.shape[-1]
    earlier = jnp.arange(width_refs)[:, None] > jnp.arange(width_refs)[None, :]
    same = owners[..., :, None] == owners[..., None, :]
    return jnp.sum(same & earlier, axis=-1)


def norm_rows(x, gain):
    scale = lax.rsqrt(jnp.mean(x * x, axis=-1, keepdims=True) + norm_eps)
    return x * scale * gain


def query_kernel(pairs, plen, heads, hd, slots, idx_ref, q_ref, gain_ref, own_ref, out_ref):
    gain = gain_ref[...]
    for two in range(heads // 2):
        parts = [
            norm_rows(q_ref[:, (2 * two + e) * hd : (2 * two + e + 1) * hd].astype(jnp.float32), gain)
            for e in range(2)
        ]
        for p in range(pairs):
            rows = jnp.concatenate([x[p * plen : (p + 1) * plen] for x in parts], axis=0)
            own_ref[p, two * 2 * plen : (two + 1) * 2 * plen, :] = rows.astype(jnp.bfloat16)

    def body(s, carry):
        out_ref[s] = own_ref[idx_ref[s]]
        return carry

    lax.fori_loop(0, slots, body, 0)


def prepare_queries(idx, queries, gain):
    pairs, plen, width = queries.shape
    hd = gain.shape[0]
    heads = width // hd
    slots = idx.shape[0]
    return pl.pallas_call(
        functools.partial(query_kernel, pairs, plen, heads, hd, slots),
        out_shape=[
            jax.ShapeDtypeStruct((pairs, heads * plen, hd), jnp.bfloat16),
            jax.ShapeDtypeStruct((slots, heads * plen, hd), jnp.bfloat16),
        ],
        in_specs=[
            pl.BlockSpec(memory_space=pltpu.SMEM),
            pl.BlockSpec(memory_space=VMEM),
            pl.BlockSpec(memory_space=VMEM),
        ],
        out_specs=[pl.BlockSpec(memory_space=VMEM)] * 2,
        compiler_params=pltpu.CompilerParams(vmem_limit_bytes=LIMIT),
    )(idx, queries.reshape(pairs * plen, width), gain.reshape(1, hd))


def project_kernel(hd, x_ref, wk_ref, wv_ref, gain_ref, k_ref, v_ref):
    x = x_ref[...]
    raw = jnp.dot(x, wk_ref[...], preferred_element_type=jnp.float32)
    for h in range(raw.shape[1] // hd):
        cols = slice(h * hd, (h + 1) * hd)
        k_ref[:, cols] = norm_rows(raw[:, cols], gain_ref[...]).astype(jnp.bfloat16)
    v_ref[...] = jnp.dot(x, wv_ref[...], preferred_element_type=jnp.float32).astype(jnp.bfloat16)


def project(x, wk, wv, gain):
    rows, width = x.shape
    kvw = wk.shape[1]
    hd = gain.shape[0]
    block = 128
    whole = pl.BlockSpec((width, kvw), lambda i: (0, 0), pipeline_mode=pl.Buffered(1))
    return pl.pallas_call(
        functools.partial(project_kernel, hd),
        grid=(rows // block,),
        out_shape=[jax.ShapeDtypeStruct((rows, kvw), jnp.bfloat16)] * 2,
        in_specs=[
            pl.BlockSpec((block, width), lambda i: (i, 0)),
            whole,
            whole,
            pl.BlockSpec((1, hd), lambda i: (0, 0)),
        ],
        out_specs=[pl.BlockSpec((block, kvw), lambda i: (i, 0))] * 2,
        compiler_params=pltpu.CompilerParams(vmem_limit_bytes=LIMIT),
    )(x, wk, wv, gain.reshape(1, hd))


def attend(q, k, v, valid, scale):
    scores = lax.dot_general(q, k, (((1,), (1,)), ((), ())), preferred_element_type=jnp.float32) * scale
    weights = jnp.where(valid, jnp.exp(scores), 0.0)
    total = jnp.sum(weights, axis=-1, keepdims=True)
    numer = jnp.dot(weights.astype(jnp.bfloat16), v, preferred_element_type=jnp.float32)
    return (numer / total).astype(jnp.bfloat16), total


def owner_kernel(per, kvh, hd, scale, slot_ref, len_ref, q_ref, k_ref, v_ref, o_ref):
    step = pl.program_id(0)
    rows = q_ref.shape[1]
    each = rows // kvh
    alen = k_ref.shape[1]
    spots = [(slice(h * each, (h + 1) * each), slice(h * hd, (h + 1) * hd)) for h in range(kvh)]
    for e in range(per):
        ref = step * per + e
        row = slot_ref[ref]
        count = len_ref[ref]
        scores = jnp.concatenate(
            [
                lax.dot_general(
                    q_ref[e, at, :], k_ref[row, :, cols], (((1,), (1,)), ((), ())),
                    preferred_element_type=jnp.float32,
                )
                for at, cols in spots
            ],
            axis=0,
        )
        position = lax.broadcasted_iota(jnp.int32, (rows, alen), 1)
        weights = jnp.where(position < count, jnp.exp(scores * scale), 0.0)
        total = jnp.sum(weights, axis=-1, keepdims=True)
        rounded = weights.astype(jnp.bfloat16)
        numer = jnp.concatenate(
            [
                jnp.dot(rounded[at], v_ref[row, :, cols], preferred_element_type=jnp.float32)
                for at, cols in spots
            ],
            axis=0,
        )
        o_ref[e, :rows, :] = (numer / total).astype(jnp.bfloat16)
        o_ref[e, rows:, :] = pack_totals(jnp.broadcast_to(total, (rows, hd)))


def pack_totals(total):
    rows, hd = total.shape
    flat = total.T[:16]
    left = [flat[:, i * hd : (i + 1) * hd] for i in range(rows // hd)]
    place = lax.broadcasted_iota(jnp.int32, (16, hd), 0)
    packed = jnp.zeros((16, hd), jnp.float32)
    at = 0
    for _ in range(3):
        for i in range(len(left)):
            term = left[i].astype(jnp.bfloat16).astype(jnp.float32)
            packed = jnp.where(place == at, term, packed)
            left[i] = left[i] - term
            at += 1
    return packed.astype(jnp.bfloat16)


def unpack_totals(packed, rows):
    hd = packed.shape[1]
    terms = packed.astype(jnp.float32)
    count = rows // hd
    flat = [
        terms[i : i + 1] + terms[count + i : count + i + 1] + terms[2 * count + i : 2 * count + i + 1]
        for i in range(count)
    ]
    return jnp.concatenate([jnp.broadcast_to(f, (hd, hd)).T for f in flat], axis=0)


def owner_attention(slot, lens, q, keys, values, hd):
    slots, rows, _ = q.shape
    _, alen, kvw = keys.shape
    per = 4
    spec = lambda shape, f: pl.BlockSpec(shape, f)
    return pl.pallas_call(
        functools.partial(owner_kernel, per, kvw // hd, hd, hd ** (-0.5)),
        grid_spec=pltpu.PrefetchScalarGridSpec(
            num_scalar_prefetch=2,
            grid=(slots // per,),
            in_specs=[
                spec((per, rows, hd), lambda i, *_: (i, 0, 0)),
                spec(keys.shape, lambda i, *_: (0, 0, 0)),
                spec(keys.shape, lambda i, *_: (0, 0, 0)),
            ],
            out_specs=spec((per, rows + 16, hd), lambda i, *_: (i, 0, 0)),
        ),
        out_shape=jax.ShapeDtypeStruct((slots, rows + 16, hd), jnp.bfloat16),
        compiler_params=pltpu.CompilerParams(vmem_limit_bytes=LIMIT),
    )(slot, lens, q, keys, values)


def combine_kernel(per, plen, kvh, hd, scale, at_ref, q_ref, k_ref, v_ref, in_ref, o_ref):
    step = pl.program_id(0)
    rows = q_ref.shape[1]
    each = rows // kvh
    keys_count = k_ref.shape[0]
    results = []
    for e in range(per):
        pair = step * per + e
        place = lax.broadcasted_iota(jnp.int32, (each, keys_count), 1)
        token = lax.broadcasted_iota(jnp.int32, (each, keys_count), 0) % plen
        valid = (place // plen == pair) & (place % plen <= token)
        numers, denoms = [], []
        for h in range(kvh):
            cols = slice(h * hd, (h + 1) * hd)
            mixed, total = attend(
                q_ref[e, h * each : (h + 1) * each, :], k_ref[:, cols], v_ref[:, cols], valid, scale
            )
            numers.append(total * mixed.astype(jnp.float32))
            denoms.append(jnp.broadcast_to(total, (each, hd)))
        numer = jnp.concatenate(numers, axis=0)
        denom = jnp.concatenate(denoms, axis=0)
        for side in range(2):
            at = at_ref[pair * 2 + side]
            total = unpack_totals(in_ref[at, rows:, :], rows)
            numer = numer + total * in_ref[at, :rows, :].astype(jnp.float32)
            denom = denom + total
        results.append(numer / denom)
    for head in range(rows // plen):
        block = jnp.concatenate([r[head * plen : (head + 1) * plen] for r in results], axis=0)
        o_ref[:, head * hd : (head + 1) * hd] = block.astype(jnp.bfloat16)


def combine(at, q, keys, values, incoming, plen, hd):
    pairs, rows, _ = q.shape
    slots = incoming.shape[0]
    kvw = keys.shape[1]
    per = 4
    heads = rows // plen
    return pl.pallas_call(
        functools.partial(combine_kernel, per, plen, kvw // hd, hd, hd ** (-0.5)),
        grid_spec=pltpu.PrefetchScalarGridSpec(
            num_scalar_prefetch=1,
            grid=(pairs // per,),
            in_specs=[
                pl.BlockSpec((per, rows, hd), lambda i, *_: (i, 0, 0)),
                pl.BlockSpec(keys.shape, lambda i, *_: (0, 0)),
                pl.BlockSpec(keys.shape, lambda i, *_: (0, 0)),
                pl.BlockSpec(incoming.shape, lambda i, *_: (0, 0, 0)),
            ],
            out_specs=pl.BlockSpec((per * plen, heads * hd), lambda i, *_: (i, 0)),
        ),
        out_shape=jax.ShapeDtypeStruct((pairs * plen, heads * hd), jnp.bfloat16),
        compiler_params=pltpu.CompilerParams(vmem_limit_bytes=LIMIT),
    )(at, q, keys, values, incoming)


def ring_kernel(
    chips, seg, wk_ref, wv_ref, ok_ref, ov_ref,
    own_sem, ring_send, ring_recv, side_send, side_recv, swap_send, swap_recv, late_send, late_recv,
):
    me = lax.axis_index("pair")
    group = lax.axis_index("groups")
    depth = wk_ref.shape[0]
    chip, core = me // 2, me % 2
    even = chip % 2
    odd_group = group % 2
    position = (1 - even) * (chip // 2) + even * (chips - 1 - chip // 2)

    def chip_at(place):
        place = (place + 2 * chips) % chips
        back = place // (chips // 2)
        return (1 - back) * 2 * place + back * (2 * (chips - 1 - place) + 1)

    right = (group, chip_at(position + 1) * 2 + core)
    left = (group, chip_at(position - 1) * 2 + core)
    sibling = (group, chip * 2 + 1 - core)
    twin = (group + 1 - 2 * odd_group, me)
    partners = (right, left)
    mesh_id = pl.DeviceIdType.MESH

    barrier = pltpu.get_barrier_semaphore()
    for other in (right, left, sibling, twin):
        pl.semaphore_signal(barrier, inc=1, device_id=other, device_id_type=mesh_id)
    own = []
    outs = (ok_ref, ov_ref)
    for w, (src, out) in enumerate(((wk_ref, ok_ref), (wv_ref, ov_ref))):
        copy = pltpu.make_async_copy(src, out.at[me], own_sem.at[w])
        copy.start()
        own.append(copy)
    for copy in own:
        copy.wait()
    pl.semaphore_wait(barrier, 4)

    ringed = pl.ds(pl.multiple_of(odd_group * seg, 16), depth - seg)
    mine = pl.ds(pl.multiple_of(odd_group * (depth - seg), 16), seg)
    other_rows = pl.ds(pl.multiple_of((1 - odd_group) * (depth - seg), 16), seg)

    def piece(w, step, on):
        return chip_at(position - step if w == 0 else position + step) * 2 + on

    def remote(block, send, recv, target):
        return pltpu.make_async_remote_copy(
            src_ref=block, dst_ref=block, send_sem=send, recv_sem=recv, device_id=target, device_id_type=mesh_id
        )

    def ring(w, step, arriving=0):
        block = outs[w].at[piece(w, step + arriving, core), ringed]
        return remote(block, ring_send.at[w, step], ring_recv.at[w, step], partners[w])

    def side(w, step, on):
        block = outs[w].at[piece(w, step, on), ringed]
        return remote(block, side_send.at[w, step], side_recv.at[w, step], sibling)

    def swap(w, step, rows):
        block = outs[w].at[piece(w, step, core), rows]
        return remote(block, swap_send.at[w, step], swap_recv.at[w, step], twin)

    def late(w, step, on):
        block = outs[w].at[piece(w, step, on), other_rows]
        return remote(block, late_send.at[w, step], late_recv.at[w, step], sibling)

    for w in range(2):
        ring(w, 0).start()
    for w in range(2):
        side(w, 0, core).start()
        late(w, 0, core).start()

    def body(step, carry):
        for w in range(2):
            ring(w, step - 1, 1).wait_recv()

            @pl.when(step < chips - 1)
            def _():
                ring(w, step).start()

            swap(w, step, mine).start()
            side(w, step, core).start()

        @pl.when(step > 1)
        def _():
            for w in range(2):
                swap(w, step - 1, other_rows).wait_recv()
                late(w, step - 1, core).start()

        return carry

    lax.fori_loop(1, chips, body, 0)
    for w in range(2):
        swap(w, chips - 1, other_rows).wait_recv()
        late(w, chips - 1, core).start()

    def drain(step, carry):
        for w in range(2):
            side(w, step, core).wait_send()
            side(w, step, 1 - core).wait_recv()
            late(w, step, core).wait_send()
            late(w, step, 1 - core).wait_recv()

            @pl.when(step < chips - 1)
            def _():
                ring(w, step).wait_send()

            @pl.when(step > 0)
            def _():
                swap(w, step, mine).wait_send()

        return carry

    lax.fori_loop(0, chips, drain, 0)


def gather_weights(w_key, w_value):
    peers = lax.axis_size("pair")
    depth, kvw = w_key.shape
    if not USE_RING:
        return tuple(lax.all_gather(w, "pair", axis=0, tiled=True) for w in (w_key, w_value))
    chips = peers // 2
    seg = max(1, round(depth // 16 * 0.35)) * 16
    hbm = pl.BlockSpec(memory_space=pl.ANY)
    out = pl.pallas_call(
        functools.partial(ring_kernel, chips, seg),
        out_shape=[jax.ShapeDtypeStruct((peers, depth, kvw), jnp.bfloat16)] * 2,
        in_specs=[hbm] * 2,
        out_specs=[hbm] * 2,
        scratch_shapes=[pltpu.SemaphoreType.DMA((2,))] + [pltpu.SemaphoreType.DMA((2, chips))] * 8,
        compiler_params=pltpu.CompilerParams(
            collective_id=0, has_side_effects=True, vmem_limit_bytes=LIMIT
        ),
    )(w_key, w_value)
    return tuple(w.reshape(peers * depth, kvw) for w in out)


def per_device(
    answer_states, prompt_states, queries, w_key, w_value, key_gain, query_gain, pair_list, answer_row, lengths
):
    device = lax.axis_index("pair")
    peers = lax.axis_size("pair")
    ans_dev, ans_len, width = answer_states.shape
    pairs_dev, prompt_len = (queries.shape[0], queries.shape[1])
    head_dim = key_gain.shape[0]
    kv_width = w_key.shape[1]
    refs = 2 * pairs_dev
    capacity = (refs + peers - 1) // peers
    slots = peers * capacity

    all_ids = pair_list.reshape(peers, refs)
    all_rows = table_lookup(answer_row, all_ids)
    all_owner = all_rows // ans_dev
    all_local = all_rows % ans_dev
    all_rank = earlier_same(all_owner)
    all_lens = table_lookup(lengths, all_ids)
    my_owner = lax.dynamic_index_in_dim(all_owner, device, 0, keepdims=False)
    my_rank = lax.dynamic_index_in_dim(all_rank, device, 0, keepdims=False)
    fetch_index = my_owner * capacity + my_rank
    slot_ids = jnp.arange(slots, dtype=jnp.int32)
    ref_match = fetch_index[None, :] == slot_ids[:, None]
    ref_pair = jnp.sum(jnp.where(ref_match, jnp.arange(refs, dtype=jnp.int32)[None, :] // 2, 0), axis=1)
    slot_range = jnp.arange(capacity, dtype=jnp.int32)
    slot_match = (all_owner == device)[:, None, :] & (all_rank[:, None, :] == slot_range[None, :, None])
    slot_local = jnp.sum(jnp.where(slot_match, all_local[:, None, :], 0), axis=-1).reshape(slots)
    slot_lens = jnp.sum(jnp.where(slot_match, all_lens[:, None, :], 0), axis=-1).reshape(slots)
    slot_lens = jnp.maximum(slot_lens, 1)

    query_own, outgoing = prepare_queries(ref_pair, queries, query_gain)
    asked = lax.all_to_all(outgoing, "pair", split_axis=0, concat_axis=0, tiled=True)
    key_full, value_full = gather_weights(w_key, w_value)
    answer_keys, answer_values = project(
        answer_states.reshape(ans_dev * ans_len, width), key_full, value_full, key_gain
    )
    mixed = owner_attention(
        slot_local,
        slot_lens,
        asked,
        answer_keys.reshape(ans_dev, ans_len, kv_width),
        answer_values.reshape(ans_dev, ans_len, kv_width),
        head_dim,
    )
    mixed_in = lax.all_to_all(mixed, "pair", split_axis=0, concat_axis=0, tiled=True)
    prompt_keys, prompt_values = project(
        prompt_states.reshape(pairs_dev * prompt_len, width), key_full, value_full, key_gain
    )
    out = combine(
        fetch_index, query_own, prompt_keys, prompt_values, mixed_in, prompt_len, head_dim
    )
    return out.reshape(queries.shape)


def solution(mesh):
    in_specs = (
        P(("groups", "pair"), None, None),
        P(("groups", "pair"), None, None),
        P(("groups", "pair"), None, None),
        P("pair", None),
        P("pair", None),
        P(),
        P(),
        P("groups", None),
        P("groups"),
        P("groups"),
    )
    out_specs = P(("groups", "pair"), None, None)
    return jax.shard_map(
        per_device, mesh=mesh, in_specs=in_specs, out_specs=out_specs, check_vma=False
    )
```

```python
import functools
import jax
import jax.numpy as jnp
from jax import lax
from jax.experimental import pallas as pl
from jax.experimental.pallas import tpu as pltpu
from jax.sharding import PartitionSpec as P

norm_eps = 1e-06
VMEM = pltpu.VMEM
LIMIT = 48 * 1024 * 1024
USE_RING = True


def table_lookup(table, indices):
    match = indices[..., None] == jnp.arange(table.shape[0], dtype=jnp.int32)
    return jnp.sum(jnp.where(match, table, 0), axis=-1)


def earlier_same(owners):
    width_refs = owners.shape[-1]
    earlier = jnp.arange(width_refs)[:, None] > jnp.arange(width_refs)[None, :]
    same = owners[..., :, None] == owners[..., None, :]
    return jnp.sum(same & earlier, axis=-1)


def norm_rows(x, gain):
    scale = lax.rsqrt(jnp.mean(x * x, axis=-1, keepdims=True) + norm_eps)
    return x * scale * gain


def query_kernel(pairs, plen, heads, hd, slots, idx_ref, q_ref, gain_ref, own_ref, out_ref):
    gain = gain_ref[...]
    for two in range(heads // 2):
        parts = [
            norm_rows(q_ref[:, (2 * two + e) * hd : (2 * two + e + 1) * hd].astype(jnp.float32), gain)
            for e in range(2)
        ]
        for p in range(pairs):
            rows = jnp.concatenate([x[p * plen : (p + 1) * plen] for x in parts], axis=0)
            own_ref[p, two * 2 * plen : (two + 1) * 2 * plen, :] = rows.astype(jnp.bfloat16)

    def body(s, carry):
        out_ref[s] = own_ref[idx_ref[s]]
        return carry

    lax.fori_loop(0, slots, body, 0)


def prepare_queries(idx, queries, gain):
    pairs, plen, width = queries.shape
    hd = gain.shape[0]
    heads = width // hd
    slots = idx.shape[0]
    return pl.pallas_call(
        functools.partial(query_kernel, pairs, plen, heads, hd, slots),
        out_shape=[
            jax.ShapeDtypeStruct((pairs, heads * plen, hd), jnp.bfloat16),
            jax.ShapeDtypeStruct((slots, heads * plen, hd), jnp.bfloat16),
        ],
        in_specs=[
            pl.BlockSpec(memory_space=pltpu.SMEM),
            pl.BlockSpec(memory_space=VMEM),
            pl.BlockSpec(memory_space=VMEM),
        ],
        out_specs=[pl.BlockSpec(memory_space=VMEM)] * 2,
        compiler_params=pltpu.CompilerParams(vmem_limit_bytes=LIMIT),
    )(idx, queries.reshape(pairs * plen, width), gain.reshape(1, hd))


def project_kernel(hd, x_ref, wk_ref, wv_ref, gain_ref, k_ref, v_ref):
    x = x_ref[...]
    raw = jnp.dot(x, wk_ref[...], preferred_element_type=jnp.float32)
    for h in range(raw.shape[1] // hd):
        cols = slice(h * hd, (h + 1) * hd)
        k_ref[:, cols] = norm_rows(raw[:, cols], gain_ref[...]).astype(jnp.bfloat16)
    v_ref[...] = jnp.dot(x, wv_ref[...], preferred_element_type=jnp.float32).astype(jnp.bfloat16)


def project(x, wk, wv, gain):
    rows, width = x.shape
    kvw = wk.shape[1]
    hd = gain.shape[0]
    block = 128
    whole = pl.BlockSpec((width, kvw), lambda i: (0, 0), pipeline_mode=pl.Buffered(1))
    return pl.pallas_call(
        functools.partial(project_kernel, hd),
        grid=(rows // block,),
        out_shape=[jax.ShapeDtypeStruct((rows, kvw), jnp.bfloat16)] * 2,
        in_specs=[
            pl.BlockSpec((block, width), lambda i: (i, 0)),
            whole,
            whole,
            pl.BlockSpec((1, hd), lambda i: (0, 0)),
        ],
        out_specs=[pl.BlockSpec((block, kvw), lambda i: (i, 0))] * 2,
        compiler_params=pltpu.CompilerParams(vmem_limit_bytes=LIMIT),
    )(x, wk, wv, gain.reshape(1, hd))


def owner_kernel(per, kvh, hd, scale, slot_ref, len_ref, q_ref, k_ref, v_ref, o_ref):
    step = pl.program_id(0)
    rows = q_ref.shape[1]
    each = rows // kvh
    alen = k_ref.shape[1]
    spots = [(slice(h * each, (h + 1) * each), slice(h * hd, (h + 1) * hd)) for h in range(kvh)]
    for e in range(per):
        ref = step * per + e
        row = slot_ref[ref]
        count = len_ref[ref]
        scores = jnp.concatenate(
            [
                lax.dot_general(
                    q_ref[e, at, :], k_ref[row, :, cols], (((1,), (1,)), ((), ())),
                    preferred_element_type=jnp.float32,
                )
                for at, cols in spots
            ],
            axis=0,
        )
        position = lax.broadcasted_iota(jnp.int32, (rows, alen), 1)
        weights = jnp.where(position < count, jnp.exp(scores * scale), 0.0)
        total = jnp.sum(weights, axis=-1, keepdims=True)
        rounded = weights.astype(jnp.bfloat16)
        numer = jnp.concatenate(
            [
                jnp.dot(rounded[at], v_ref[row, :, cols], preferred_element_type=jnp.float32)
                for at, cols in spots
            ],
            axis=0,
        )
        o_ref[e, :rows, :] = (numer / total).astype(jnp.bfloat16)
        o_ref[e, rows:, :] = pack_totals(jnp.broadcast_to(total, (rows, hd)))


def pack_totals(total):
    rows, hd = total.shape
    flat = total.T[:16]
    left = [flat[:, i * hd : (i + 1) * hd] for i in range(rows // hd)]
    place = lax.broadcasted_iota(jnp.int32, (16, hd), 0)
    packed = jnp.zeros((16, hd), jnp.float32)
    at = 0
    for _ in range(3):
        for i in range(len(left)):
            term = left[i].astype(jnp.bfloat16).astype(jnp.float32)
            packed = jnp.where(place == at, term, packed)
            left[i] = left[i] - term
            at += 1
    return packed.astype(jnp.bfloat16)


def unpack_totals(packed, rows):
    hd = packed.shape[1]
    terms = packed.astype(jnp.float32)
    count = rows // hd
    flat = [
        terms[i : i + 1] + terms[count + i : count + i + 1] + terms[2 * count + i : 2 * count + i + 1]
        for i in range(count)
    ]
    return jnp.concatenate([jnp.broadcast_to(f, (hd, hd)).T for f in flat], axis=0)


def owner_attention(slot, lens, q, keys, values, hd):
    slots, rows, _ = q.shape
    _, alen, kvw = keys.shape
    per = 4
    spec = lambda shape, f: pl.BlockSpec(shape, f)
    return pl.pallas_call(
        functools.partial(owner_kernel, per, kvw // hd, hd, hd ** (-0.5)),
        grid_spec=pltpu.PrefetchScalarGridSpec(
            num_scalar_prefetch=2,
            grid=(slots // per,),
            in_specs=[
                spec((per, rows, hd), lambda i, *_: (i, 0, 0)),
                spec(keys.shape, lambda i, *_: (0, 0, 0)),
                spec(keys.shape, lambda i, *_: (0, 0, 0)),
            ],
            out_specs=spec((per, rows + 16, hd), lambda i, *_: (i, 0, 0)),
        ),
        out_shape=jax.ShapeDtypeStruct((slots, rows + 16, hd), jnp.bfloat16),
        compiler_params=pltpu.CompilerParams(vmem_limit_bytes=LIMIT),
    )(slot, lens, q, keys, values)


def prompt_kernel(per, plen, kvh, hd, scale, q_ref, k_ref, v_ref, n_ref, t_ref):
    step = pl.program_id(0)
    rows = q_ref.shape[1]
    each = rows // kvh
    keys_count = k_ref.shape[0]
    spots = [(slice(h * each, (h + 1) * each), slice(h * hd, (h + 1) * hd)) for h in range(kvh)]
    for e in range(per):
        pair = step * per + e
        place = lax.broadcasted_iota(jnp.int32, (rows, keys_count), 1)
        token = lax.broadcasted_iota(jnp.int32, (rows, keys_count), 0) % plen
        valid = (place >= pair * plen) & (place <= pair * plen + token)
        scores = jnp.concatenate(
            [
                lax.dot_general(
                    q_ref[e, at, :], k_ref[:, cols], (((1,), (1,)), ((), ())),
                    preferred_element_type=jnp.float32,
                )
                for at, cols in spots
            ],
            axis=0,
        )
        weights = jnp.where(valid, jnp.exp(scores * scale), 0.0)
        total = jnp.sum(weights, axis=-1, keepdims=True)
        rounded = weights.astype(jnp.bfloat16)
        numer = jnp.concatenate(
            [jnp.dot(rounded[at], v_ref[:, cols], preferred_element_type=jnp.float32) for at, cols in spots],
            axis=0,
        )
        mixed = (numer / total).astype(jnp.bfloat16).astype(jnp.float32)
        n_ref[e] = total * mixed
        t_ref[e] = jnp.broadcast_to(total, (rows, hd))


def prompt_attention(q, keys, values, plen, hd):
    pairs, rows, _ = q.shape
    kvw = keys.shape[1]
    per = 4
    block = pl.BlockSpec((per, rows, hd), lambda i: (i, 0, 0))
    full = pl.BlockSpec(keys.shape, lambda i: (0, 0))
    return pl.pallas_call(
        functools.partial(prompt_kernel, per, plen, kvw // hd, hd, hd ** (-0.5)),
        grid=(pairs // per,),
        in_specs=[block, full, full],
        out_specs=[block] * 2,
        out_shape=[jax.ShapeDtypeStruct((pairs, rows, hd), jnp.float32)] * 2,
        compiler_params=pltpu.CompilerParams(vmem_limit_bytes=LIMIT),
    )(q, keys, values)


def combine_kernel(per, plen, hd, at_ref, n_ref, t_ref, in_ref, o_ref):
    step = pl.program_id(0)
    rows = n_ref.shape[1]
    results = []
    for e in range(per):
        numer = n_ref[e]
        denom = t_ref[e]
        for side in range(2):
            at = at_ref[(step * per + e) * 2 + side]
            total = unpack_totals(in_ref[at, rows:, :], rows)
            numer = numer + total * in_ref[at, :rows, :].astype(jnp.float32)
            denom = denom + total
        results.append(numer / denom)
    for head in range(rows // plen):
        block = jnp.concatenate([r[head * plen : (head + 1) * plen] for r in results], axis=0)
        o_ref[:, head * hd : (head + 1) * hd] = block.astype(jnp.bfloat16)


def combine(at, numer, denom, incoming, plen, hd):
    pairs, rows, _ = numer.shape
    per = 4
    heads = rows // plen
    block = pl.BlockSpec((per, rows, hd), lambda i, *_: (i, 0, 0))
    return pl.pallas_call(
        functools.partial(combine_kernel, per, plen, hd),
        grid_spec=pltpu.PrefetchScalarGridSpec(
            num_scalar_prefetch=1,
            grid=(pairs // per,),
            in_specs=[block, block, pl.BlockSpec(incoming.shape, lambda i, *_: (0, 0, 0))],
            out_specs=pl.BlockSpec((per * plen, heads * hd), lambda i, *_: (i, 0)),
        ),
        out_shape=jax.ShapeDtypeStruct((pairs * plen, heads * hd), jnp.bfloat16),
        compiler_params=pltpu.CompilerParams(vmem_limit_bytes=LIMIT),
    )(at, numer, denom, incoming)


def ring_kernel(
    chips, seg, wk_ref, wv_ref, ok_ref, ov_ref,
    own_sem, ring_send, ring_recv, side_send, side_recv, swap_send, swap_recv, late_send, late_recv,
):
    me = lax.axis_index("pair")
    group = lax.axis_index("groups")
    depth = wk_ref.shape[0]
    chip, core = me // 2, me % 2
    even = chip % 2
    odd_group = group % 2
    position = (1 - even) * (chip // 2) + even * (chips - 1 - chip // 2)

    def chip_at(place):
        place = (place + 2 * chips) % chips
        back = place // (chips // 2)
        return (1 - back) * 2 * place + back * (2 * (chips - 1 - place) + 1)

    right = (group, chip_at(position + 1) * 2 + core)
    left = (group, chip_at(position - 1) * 2 + core)
    sibling = (group, chip * 2 + 1 - core)
    twin = (group + 1 - 2 * odd_group, me)
    partners = (right, left)
    mesh_id = pl.DeviceIdType.MESH

    barrier = pltpu.get_barrier_semaphore()
    for other in (right, left, sibling, twin):
        pl.semaphore_signal(barrier, inc=1, device_id=other, device_id_type=mesh_id)
    own = []
    outs = (ok_ref, ov_ref)
    for w, (src, out) in enumerate(((wk_ref, ok_ref), (wv_ref, ov_ref))):
        copy = pltpu.make_async_copy(src, out.at[me], own_sem.at[w])
        copy.start()
        own.append(copy)
    for copy in own:
        copy.wait()
    pl.semaphore_wait(barrier, 4)

    first = ((depth - seg) // 16 + 1) // 2 * 16
    chunks = tuple(
        pl.ds(pl.multiple_of(odd_group * seg + start, 16), size)
        for start, size in ((0, first), (first, depth - seg - first))
    )
    mine = pl.ds(pl.multiple_of(odd_group * (depth - seg), 16), seg)
    other_rows = pl.ds(pl.multiple_of((1 - odd_group) * (depth - seg), 16), seg)

    def piece(w, step, on):
        return chip_at(position - step if w == 0 else position + step) * 2 + on

    def remote(block, send, recv, target):
        return pltpu.make_async_remote_copy(
            src_ref=block, dst_ref=block, send_sem=send, recv_sem=recv, device_id=target, device_id_type=mesh_id
        )

    def ring(w, step, c, arriving=0):
        block = outs[w].at[piece(w, step + arriving, core), chunks[c]]
        at = 2 * step + c
        return remote(block, ring_send.at[w, at], ring_recv.at[w, at], partners[w])

    def side(w, step, c, on):
        block = outs[w].at[piece(w, step, on), chunks[c]]
        at = 2 * step + c
        return remote(block, side_send.at[w, at], side_recv.at[w, at], sibling)

    def swap(w, step, rows):
        block = outs[w].at[piece(w, step, core), rows]
        return remote(block, swap_send.at[w, step], swap_recv.at[w, step], twin)

    def late(w, step, on):
        block = outs[w].at[piece(w, step, on), other_rows]
        return remote(block, late_send.at[w, step], late_recv.at[w, step], sibling)

    both = [(c, w) for c in range(2) for w in range(2)]
    for c, w in both:
        ring(w, 0, c).start()
    for c, w in both:
        side(w, 0, c, core).start()
    for w in range(2):
        late(w, 0, core).start()

    def hand_over(step):
        for w in range(2):
            swap(w, step, other_rows).wait_recv()
            late(w, step, core).start()

    lag = 3

    def body(step, carry):
        for c, w in both:
            ring(w, step - 1, c, 1).wait_recv()

            @pl.when(step < chips - 1)
            def _():
                ring(w, step, c).start()

            side(w, step, c, core).start()
        for w in range(2):
            swap(w, step, mine).start()

        @pl.when(step > lag)
        def _():
            hand_over(step - lag)

        return carry

    lax.fori_loop(1, chips, body, 0)

    def finish(step, carry):
        hand_over(step)
        return carry

    lax.fori_loop(chips - lag, chips, finish, 0)

    def drain(step, carry):
        for c, w in both:
            side(w, step, c, core).wait_send()
            side(w, step, c, 1 - core).wait_recv()

            @pl.when(step < chips - 1)
            def _():
                ring(w, step, c).wait_send()

        for w in range(2):
            late(w, step, core).wait_send()
            late(w, step, 1 - core).wait_recv()

            @pl.when(step > 0)
            def _():
                swap(w, step, mine).wait_send()

        return carry

    lax.fori_loop(0, chips, drain, 0)


def gather_weights(w_key, w_value):
    peers = lax.axis_size("pair")
    depth, kvw = w_key.shape
    if not USE_RING:
        return tuple(lax.all_gather(w, "pair", axis=0, tiled=True) for w in (w_key, w_value))
    chips = peers // 2
    seg = max(1, round(depth // 16 * 0.35)) * 16
    hbm = pl.BlockSpec(memory_space=pl.ANY)
    out = pl.pallas_call(
        functools.partial(ring_kernel, chips, seg),
        out_shape=[jax.ShapeDtypeStruct((peers, depth, kvw), jnp.bfloat16)] * 2,
        in_specs=[hbm] * 2,
        out_specs=[hbm] * 2,
        scratch_shapes=[pltpu.SemaphoreType.DMA((2,))] + [pltpu.SemaphoreType.DMA((2, 2 * chips))] * 8,
        compiler_params=pltpu.CompilerParams(
            collective_id=0, has_side_effects=True, vmem_limit_bytes=LIMIT
        ),
    )(w_key, w_value)
    return tuple(w.reshape(peers * depth, kvw) for w in out)


def per_device(
    answer_states, prompt_states, queries, w_key, w_value, key_gain, query_gain, pair_list, answer_row, lengths
):
    device = lax.axis_index("pair")
    peers = lax.axis_size("pair")
    ans_dev, ans_len, width = answer_states.shape
    pairs_dev, prompt_len = (queries.shape[0], queries.shape[1])
    head_dim = key_gain.shape[0]
    kv_width = w_key.shape[1]
    refs = 2 * pairs_dev
    capacity = (refs + peers - 1) // peers
    slots = peers * capacity

    all_ids = pair_list.reshape(peers, refs)
    all_rows = table_lookup(answer_row, all_ids)
    all_owner = all_rows // ans_dev
    all_local = all_rows % ans_dev
    all_rank = earlier_same(all_owner)
    all_lens = table_lookup(lengths, all_ids)
    my_owner = lax.dynamic_index_in_dim(all_owner, device, 0, keepdims=False)
    my_rank = lax.dynamic_index_in_dim(all_rank, device, 0, keepdims=False)
    fetch_index = my_owner * capacity + my_rank
    slot_ids = jnp.arange(slots, dtype=jnp.int32)
    ref_match = fetch_index[None, :] == slot_ids[:, None]
    ref_pair = jnp.sum(jnp.where(ref_match, jnp.arange(refs, dtype=jnp.int32)[None, :] // 2, 0), axis=1)
    slot_range = jnp.arange(capacity, dtype=jnp.int32)
    slot_match = (all_owner == device)[:, None, :] & (all_rank[:, None, :] == slot_range[None, :, None])
    slot_local = jnp.sum(jnp.where(slot_match, all_local[:, None, :], 0), axis=-1).reshape(slots)
    slot_lens = jnp.sum(jnp.where(slot_match, all_lens[:, None, :], 0), axis=-1).reshape(slots)
    slot_lens = jnp.maximum(slot_lens, 1)

    query_own, outgoing = prepare_queries(ref_pair, queries, query_gain)
    asked = lax.all_to_all(outgoing, "pair", split_axis=0, concat_axis=0, tiled=True)
    key_full, value_full = gather_weights(w_key, w_value)
    answer_keys, answer_values = project(
        answer_states.reshape(ans_dev * ans_len, width), key_full, value_full, key_gain
    )
    mixed = owner_attention(
        slot_local,
        slot_lens,
        asked,
        answer_keys.reshape(ans_dev, ans_len, kv_width),
        answer_values.reshape(ans_dev, ans_len, kv_width),
        head_dim,
    )
    mixed_in = lax.all_to_all(mixed, "pair", split_axis=0, concat_axis=0, tiled=True)
    prompt_keys, prompt_values = project(
        prompt_states.reshape(pairs_dev * prompt_len, width), key_full, value_full, key_gain
    )
    own_numer, own_total = prompt_attention(query_own, prompt_keys, prompt_values, prompt_len, head_dim)
    out = combine(fetch_index, own_numer, own_total, mixed_in, prompt_len, head_dim)
    return out.reshape(queries.shape)


def solution(mesh):
    in_specs = (
        P(("groups", "pair"), None, None),
        P(("groups", "pair"), None, None),
        P(("groups", "pair"), None, None),
        P("pair", None),
        P("pair", None),
        P(),
        P(),
        P("groups", None),
        P("groups"),
        P("groups"),
    )
    out_specs = P(("groups", "pair"), None, None)
    return jax.shard_map(
        per_device, mesh=mesh, in_specs=in_specs, out_specs=out_specs, check_vma=False
    )
```

```python
import functools
import jax
import jax.numpy as jnp
from jax import lax
from jax.experimental import pallas as pl
from jax.experimental.pallas import tpu as pltpu
from jax.sharding import PartitionSpec as P

norm_eps = 1e-06
VMEM = pltpu.VMEM
LIMIT = 48 * 1024 * 1024


def table_lookup(table, indices):
    match = indices[..., None] == jnp.arange(table.shape[0], dtype=jnp.int32)
    return jnp.sum(jnp.where(match, table, 0), axis=-1)


def earlier_same(owners):
    width_refs = owners.shape[-1]
    earlier = jnp.arange(width_refs)[:, None] > jnp.arange(width_refs)[None, :]
    same = owners[..., :, None] == owners[..., None, :]
    return jnp.sum(same & earlier, axis=-1)


def norm_rows(x, gain):
    scale = lax.rsqrt(jnp.mean(x * x, axis=-1, keepdims=True) + norm_eps)
    return x * scale * gain


def query_kernel(pairs, plen, heads, hd, slots, idx_ref, q_ref, gain_ref, own_ref, out_ref):
    gain = gain_ref[...]
    for two in range(heads // 2):
        parts = [
            norm_rows(q_ref[:, (2 * two + e) * hd : (2 * two + e + 1) * hd].astype(jnp.float32), gain)
            for e in range(2)
        ]
        for p in range(pairs):
            rows = jnp.concatenate([x[p * plen : (p + 1) * plen] for x in parts], axis=0)
            own_ref[p, two * 2 * plen : (two + 1) * 2 * plen, :] = rows.astype(jnp.bfloat16)

    def body(s, carry):
        out_ref[s] = own_ref[idx_ref[s]]
        return carry

    lax.fori_loop(0, slots, body, 0)


def prepare_queries(idx, queries, gain):
    pairs, plen, width = queries.shape
    hd = gain.shape[0]
    heads = width // hd
    slots = idx.shape[0]
    return pl.pallas_call(
        functools.partial(query_kernel, pairs, plen, heads, hd, slots),
        out_shape=[
            jax.ShapeDtypeStruct((pairs, heads * plen, hd), jnp.bfloat16),
            jax.ShapeDtypeStruct((slots, heads * plen, hd), jnp.bfloat16),
        ],
        in_specs=[
            pl.BlockSpec(memory_space=pltpu.SMEM),
            pl.BlockSpec(memory_space=VMEM),
            pl.BlockSpec(memory_space=VMEM),
        ],
        out_specs=[pl.BlockSpec(memory_space=VMEM)] * 2,
        compiler_params=pltpu.CompilerParams(vmem_limit_bytes=LIMIT),
    )(idx, queries.reshape(pairs * plen, width), gain.reshape(1, hd))


def project_kernel(hd, x_ref, wk_ref, wv_ref, gain_ref, k_ref, v_ref):
    x = x_ref[...]
    raw = jnp.dot(x, wk_ref[...], preferred_element_type=jnp.float32)
    for h in range(raw.shape[1] // hd):
        cols = slice(h * hd, (h + 1) * hd)
        k_ref[:, cols] = norm_rows(raw[:, cols], gain_ref[...]).astype(jnp.bfloat16)
    v_ref[...] = jnp.dot(x, wv_ref[...], preferred_element_type=jnp.float32).astype(jnp.bfloat16)


def project(x, wk, wv, gain):
    rows, width = x.shape
    kvw = wk.shape[1]
    hd = gain.shape[0]
    block = 128
    whole = pl.BlockSpec((width, kvw), lambda i: (0, 0), pipeline_mode=pl.Buffered(1))
    return pl.pallas_call(
        functools.partial(project_kernel, hd),
        grid=(rows // block,),
        out_shape=[jax.ShapeDtypeStruct((rows, kvw), jnp.bfloat16)] * 2,
        in_specs=[
            pl.BlockSpec((block, width), lambda i: (i, 0)),
            whole,
            whole,
            pl.BlockSpec((1, hd), lambda i: (0, 0)),
        ],
        out_specs=[pl.BlockSpec((block, kvw), lambda i: (i, 0))] * 2,
        compiler_params=pltpu.CompilerParams(vmem_limit_bytes=LIMIT),
    )(x, wk, wv, gain.reshape(1, hd))


def owner_kernel(per, kvh, hd, scale, slot_ref, len_ref, q_ref, k_ref, v_ref, o_ref):
    step = pl.program_id(0)
    rows = q_ref.shape[1]
    each = rows // kvh
    alen = k_ref.shape[1]
    spots = [(slice(h * each, (h + 1) * each), slice(h * hd, (h + 1) * hd)) for h in range(kvh)]
    for e in range(per):
        ref = step * per + e
        row = slot_ref[ref]
        count = len_ref[ref]
        scores = jnp.concatenate(
            [
                lax.dot_general(
                    q_ref[e, at, :], k_ref[row, :, cols], (((1,), (1,)), ((), ())),
                    preferred_element_type=jnp.float32,
                )
                for at, cols in spots
            ],
            axis=0,
        )
        position = lax.broadcasted_iota(jnp.int32, (rows, alen), 1)
        weights = jnp.where(position < count, jnp.exp(scores * scale), 0.0)
        total = jnp.sum(weights, axis=-1, keepdims=True)
        rounded = weights.astype(jnp.bfloat16)
        numer = jnp.concatenate(
            [
                jnp.dot(rounded[at], v_ref[row, :, cols], preferred_element_type=jnp.float32)
                for at, cols in spots
            ],
            axis=0,
        )
        o_ref[e, :rows, :] = (numer / total).astype(jnp.bfloat16)
        o_ref[e, rows:, :] = pack_totals(jnp.broadcast_to(total, (rows, hd)))


def pack_totals(total):
    rows, hd = total.shape
    flat = total.T[:16]
    left = [flat[:, i * hd : (i + 1) * hd] for i in range(rows // hd)]
    place = lax.broadcasted_iota(jnp.int32, (16, hd), 0)
    packed = jnp.zeros((16, hd), jnp.float32)
    at = 0
    for _ in range(3):
        for i in range(len(left)):
            term = left[i].astype(jnp.bfloat16).astype(jnp.float32)
            packed = jnp.where(place == at, term, packed)
            left[i] = left[i] - term
            at += 1
    return packed.astype(jnp.bfloat16)


def unpack_totals(packed, rows):
    hd = packed.shape[1]
    terms = packed.astype(jnp.float32)
    count = rows // hd
    flat = [
        terms[i : i + 1] + terms[count + i : count + i + 1] + terms[2 * count + i : 2 * count + i + 1]
        for i in range(count)
    ]
    return jnp.concatenate([jnp.broadcast_to(f, (hd, hd)).T for f in flat], axis=0)


def owner_attention(slot, lens, q, keys, values, hd):
    slots, rows, _ = q.shape
    _, alen, kvw = keys.shape
    per = 4
    spec = lambda shape, f: pl.BlockSpec(shape, f)
    return pl.pallas_call(
        functools.partial(owner_kernel, per, kvw // hd, hd, hd ** (-0.5)),
        grid_spec=pltpu.PrefetchScalarGridSpec(
            num_scalar_prefetch=2,
            grid=(slots // per,),
            in_specs=[
                spec((per, rows, hd), lambda i, *_: (i, 0, 0)),
                spec(keys.shape, lambda i, *_: (0, 0, 0)),
                spec(keys.shape, lambda i, *_: (0, 0, 0)),
            ],
            out_specs=spec((per, rows + 16, hd), lambda i, *_: (i, 0, 0)),
        ),
        out_shape=jax.ShapeDtypeStruct((slots, rows + 16, hd), jnp.bfloat16),
        compiler_params=pltpu.CompilerParams(vmem_limit_bytes=LIMIT),
    )(slot, lens, q, keys, values)


def prompt_kernel(per, plen, kvh, hd, scale, q_ref, k_ref, v_ref, n_ref, t_ref):
    step = pl.program_id(0)
    rows = q_ref.shape[1]
    each = rows // kvh
    keys_count = k_ref.shape[0]
    spots = [(slice(h * each, (h + 1) * each), slice(h * hd, (h + 1) * hd)) for h in range(kvh)]
    for e in range(per):
        pair = step * per + e
        place = lax.broadcasted_iota(jnp.int32, (rows, keys_count), 1)
        token = lax.broadcasted_iota(jnp.int32, (rows, keys_count), 0) % plen
        valid = (place >= pair * plen) & (place <= pair * plen + token)
        scores = jnp.concatenate(
            [
                lax.dot_general(
                    q_ref[e, at, :], k_ref[:, cols], (((1,), (1,)), ((), ())),
                    preferred_element_type=jnp.float32,
                )
                for at, cols in spots
            ],
            axis=0,
        )
        weights = jnp.where(valid, jnp.exp(scores * scale), 0.0)
        total = jnp.sum(weights, axis=-1, keepdims=True)
        rounded = weights.astype(jnp.bfloat16)
        numer = jnp.concatenate(
            [jnp.dot(rounded[at], v_ref[:, cols], preferred_element_type=jnp.float32) for at, cols in spots],
            axis=0,
        )
        mixed = (numer / total).astype(jnp.bfloat16).astype(jnp.float32)
        n_ref[e] = total * mixed
        t_ref[e] = jnp.broadcast_to(total, (rows, hd))


def prompt_attention(q, keys, values, plen, hd):
    pairs, rows, _ = q.shape
    kvw = keys.shape[1]
    per = 4
    block = pl.BlockSpec((per, rows, hd), lambda i: (i, 0, 0))
    full = pl.BlockSpec(keys.shape, lambda i: (0, 0))
    return pl.pallas_call(
        functools.partial(prompt_kernel, per, plen, kvw // hd, hd, hd ** (-0.5)),
        grid=(pairs // per,),
        in_specs=[block, full, full],
        out_specs=[block] * 2,
        out_shape=[jax.ShapeDtypeStruct((pairs, rows, hd), jnp.float32)] * 2,
        compiler_params=pltpu.CompilerParams(vmem_limit_bytes=LIMIT),
    )(q, keys, values)


def combine_kernel(per, plen, hd, at_ref, n_ref, t_ref, in_ref, o_ref):
    step = pl.program_id(0)
    rows = n_ref.shape[1]
    results = []
    for e in range(per):
        numer = n_ref[e]
        denom = t_ref[e]
        for side in range(2):
            at = at_ref[(step * per + e) * 2 + side]
            total = unpack_totals(in_ref[at, rows:, :], rows)
            numer = numer + total * in_ref[at, :rows, :].astype(jnp.float32)
            denom = denom + total
        results.append(numer / denom)
    for head in range(rows // plen):
        block = jnp.concatenate([r[head * plen : (head + 1) * plen] for r in results], axis=0)
        o_ref[:, head * hd : (head + 1) * hd] = block.astype(jnp.bfloat16)


def combine(at, numer, denom, incoming, plen, hd):
    pairs, rows, _ = numer.shape
    per = 4
    heads = rows // plen
    block = pl.BlockSpec((per, rows, hd), lambda i, *_: (i, 0, 0))
    return pl.pallas_call(
        functools.partial(combine_kernel, per, plen, hd),
        grid_spec=pltpu.PrefetchScalarGridSpec(
            num_scalar_prefetch=1,
            grid=(pairs // per,),
            in_specs=[block, block, pl.BlockSpec(incoming.shape, lambda i, *_: (0, 0, 0))],
            out_specs=pl.BlockSpec((per * plen, heads * hd), lambda i, *_: (i, 0)),
        ),
        out_shape=jax.ShapeDtypeStruct((pairs * plen, heads * hd), jnp.bfloat16),
        compiler_params=pltpu.CompilerParams(vmem_limit_bytes=LIMIT),
    )(at, numer, denom, incoming)


def ring_kernel(
    chips, seg, hd, wk_ref, wv_ref, xa_ref, xp_ref, gain_ref, ak_ref, av_ref, pk_ref, pv_ref,
    keys_buf, values_buf, x_buf, key_acc, value_acc, own_sem, x_sem,
    ring_send, ring_recv, side_send, side_recv, swap_send, swap_recv, late_send, late_recv,
):
    me = lax.axis_index("pair")
    group = lax.axis_index("groups")
    depth = wk_ref.shape[0]
    chip, core = me // 2, me % 2
    even = chip % 2
    odd_group = group % 2
    position = (1 - even) * (chip // 2) + even * (chips - 1 - chip // 2)

    def chip_at(place):
        place = (place + 2 * chips) % chips
        back = place // (chips // 2)
        return (1 - back) * 2 * place + back * (2 * (chips - 1 - place) + 1)

    right = (group, chip_at(position + 1) * 2 + core)
    left = (group, chip_at(position - 1) * 2 + core)
    sibling = (group, chip * 2 + 1 - core)
    twin = (group + 1 - 2 * odd_group, me)
    partners = (right, left)
    mesh_id = pl.DeviceIdType.MESH

    barrier = pltpu.get_barrier_semaphore()
    for other in (right, left, sibling, twin):
        pl.semaphore_signal(barrier, inc=1, device_id=other, device_id_type=mesh_id)
    own = []
    outs = (keys_buf, values_buf)
    accs = (key_acc, value_acc)
    for w, (src, out) in enumerate(((wk_ref, keys_buf), (wv_ref, values_buf))):
        place = pl.ds(pl.multiple_of(core * depth, 16), depth)
        copy = pltpu.make_async_copy(src, out.at[chip, place], own_sem.at[w])
        copy.start()
        own.append(copy)
    answers = xa_ref.shape[0]
    total_rows = x_buf.shape[0]
    x_copies = (
        pltpu.make_async_copy(xa_ref, x_buf.at[:answers], x_sem.at[0]),
        pltpu.make_async_copy(xp_ref, x_buf.at[answers:], x_sem.at[1]),
    )
    for copy in x_copies:
        copy.start()
    for copy in own:
        copy.wait()
    pl.semaphore_wait(barrier, 4)

    first = ((depth - seg) // 16 + 1) // 2 * 16
    pieces = ((odd_group * seg, first), (odd_group * seg + first, depth - seg - first))
    mine = (odd_group * (depth - seg), seg)
    other_rows = ((1 - odd_group) * (depth - seg), seg)

    def block_of(w, step, on, rows):
        at = chip_at(position - step if w == 0 else position + step)
        start, size = rows
        return outs[w].at[at, pl.ds(pl.multiple_of(on * depth + start, 16), size)]

    def remote(block, send, recv, target):
        return pltpu.make_async_remote_copy(
            src_ref=block, dst_ref=block, send_sem=send, recv_sem=recv, device_id=target, device_id_type=mesh_id
        )

    def ring(w, step, c, arriving=0):
        block = block_of(w, step + arriving, core, pieces[c])
        at = 2 * step + c
        return remote(block, ring_send.at[w, at], ring_recv.at[w, at], partners[w])

    def side(w, step, c, on):
        block = block_of(w, step, on, pieces[c])
        at = 2 * step + c
        return remote(block, side_send.at[w, at], side_recv.at[w, at], sibling)

    def swap(w, step, rows):
        block = block_of(w, step, core, rows)
        return remote(block, swap_send.at[w, step], swap_recv.at[w, step], twin)

    def late(w, step, on):
        block = block_of(w, step, on, other_rows)
        return remote(block, late_send.at[w, step], late_recv.at[w, step], sibling)

    both = [(c, w) for c in range(2) for w in range(2)]
    for c, w in both:
        ring(w, 0, c).start()
    for c, w in both:
        side(w, 0, c, core).start()
    for w in range(2):
        late(w, 0, core).start()

    def hand_over(step):
        for w in range(2):
            swap(w, step, other_rows).wait_recv()
            late(w, step, core).start()

    lag = 2
    for copy in x_copies:
        copy.wait()
    for acc in accs:
        acc[...] = jnp.zeros_like(acc)
    half = total_rows // 2

    def multiply(step):
        for w in range(2):
            for c in range(2):
                side(w, step, c, 1 - core).wait_recv()
            late(w, step, 1 - core).wait_recv()
            at = chip_at(position - step if w == 0 else position + step)
            cols = pl.ds(pl.multiple_of(at * 2 * depth, 128), 2 * depth)

            def part(i, carry):
                rows = pl.ds(pl.multiple_of(i * half, 16), half)
                accs[w][rows, :] += jnp.dot(
                    x_buf[rows, cols], outs[w][at], preferred_element_type=jnp.float32
                )
                return carry

            lax.fori_loop(0, 2, part, 0)

    def body(step, carry):
        for c, w in both:
            ring(w, step - 1, c, 1).wait_recv()

            @pl.when(step < chips - 1)
            def _():
                ring(w, step, c).start()

            side(w, step, c, core).start()
        for w in range(2):
            swap(w, step, mine).start()

        @pl.when(step > lag)
        def _():
            hand_over(step - lag)

        @pl.when(step > lag)
        def _():
            multiply(step - lag - 1)

        return carry

    lax.fori_loop(1, chips, body, 0)

    def finish(step, carry):
        hand_over(step)
        return carry

    lax.fori_loop(chips - lag, chips, finish, 0)

    def rest(step, carry):
        multiply(step)
        return carry

    lax.fori_loop(chips - lag - 1, chips, rest, 0)

    block = 128
    for i in range(total_rows // block):
        rows = slice(i * block, (i + 1) * block)
        inside = i * block < answers
        to_k, to_v = (ak_ref, av_ref) if inside else (pk_ref, pv_ref)
        to = slice(i * block - (0 if inside else answers), (i + 1) * block - (0 if inside else answers))
        for h in range(key_acc.shape[1] // hd):
            cols = slice(h * hd, (h + 1) * hd)
            to_k[to, cols] = norm_rows(key_acc[rows, cols], gain_ref[...]).astype(jnp.bfloat16)
        to_v[to, :] = value_acc[rows, :].astype(jnp.bfloat16)

    def drain(step, carry):
        for c, w in both:
            side(w, step, c, core).wait_send()

            @pl.when(step < chips - 1)
            def _():
                ring(w, step, c).wait_send()

        for w in range(2):
            late(w, step, core).wait_send()

            @pl.when(step > 0)
            def _():
                swap(w, step, mine).wait_send()

        return carry

    lax.fori_loop(0, chips, drain, 0)


def encode(w_key, w_value, answer_x, prompt_x, gain):
    peers = lax.axis_size("pair")
    depth, kvw = w_key.shape
    hd = gain.shape[0]
    if 2 * depth % 128:
        key_full, value_full = (lax.all_gather(w, "pair", axis=0, tiled=True) for w in (w_key, w_value))
        return (
            *project(answer_x, key_full, value_full, gain),
            *project(prompt_x, key_full, value_full, gain),
        )
    chips = peers // 2
    seg = max(1, round(depth // 16 * 0.35)) * 16
    answers, width = answer_x.shape
    prompts = prompt_x.shape[0]
    anywhere = pl.BlockSpec(memory_space=pl.ANY)
    vmem = pl.BlockSpec(memory_space=VMEM)
    dma = pltpu.SemaphoreType.DMA
    return pl.pallas_call(
        functools.partial(ring_kernel, chips, seg, hd),
        out_shape=[jax.ShapeDtypeStruct((n, kvw), jnp.bfloat16) for n in (answers, answers, prompts, prompts)],
        in_specs=[anywhere] * 4 + [vmem],
        out_specs=[vmem] * 4,
        scratch_shapes=[VMEM((chips, 2 * depth, kvw), jnp.bfloat16)] * 2
        + [VMEM((answers + prompts, width), jnp.bfloat16)]
        + [VMEM((answers + prompts, kvw), jnp.float32)] * 2
        + [dma((2,))] * 2
        + [dma((2, 2 * chips))] * 8,
        compiler_params=pltpu.CompilerParams(
            collective_id=0, has_side_effects=True, vmem_limit_bytes=LIMIT
        ),
    )(w_key, w_value, answer_x, prompt_x, gain.reshape(1, hd))


def per_device(
    answer_states, prompt_states, queries, w_key, w_value, key_gain, query_gain, pair_list, answer_row, lengths
):
    device = lax.axis_index("pair")
    peers = lax.axis_size("pair")
    ans_dev, ans_len, width = answer_states.shape
    pairs_dev, prompt_len = (queries.shape[0], queries.shape[1])
    head_dim = key_gain.shape[0]
    kv_width = w_key.shape[1]
    refs = 2 * pairs_dev
    capacity = (refs + peers - 1) // peers
    slots = peers * capacity

    all_ids = pair_list.reshape(peers, refs)
    all_rows = table_lookup(answer_row, all_ids)
    all_owner = all_rows // ans_dev
    all_local = all_rows % ans_dev
    all_rank = earlier_same(all_owner)
    all_lens = table_lookup(lengths, all_ids)
    my_owner = lax.dynamic_index_in_dim(all_owner, device, 0, keepdims=False)
    my_rank = lax.dynamic_index_in_dim(all_rank, device, 0, keepdims=False)
    fetch_index = my_owner * capacity + my_rank
    slot_ids = jnp.arange(slots, dtype=jnp.int32)
    ref_match = fetch_index[None, :] == slot_ids[:, None]
    ref_pair = jnp.sum(jnp.where(ref_match, jnp.arange(refs, dtype=jnp.int32)[None, :] // 2, 0), axis=1)
    slot_range = jnp.arange(capacity, dtype=jnp.int32)
    slot_match = (all_owner == device)[:, None, :] & (all_rank[:, None, :] == slot_range[None, :, None])
    slot_local = jnp.sum(jnp.where(slot_match, all_local[:, None, :], 0), axis=-1).reshape(slots)
    slot_lens = jnp.sum(jnp.where(slot_match, all_lens[:, None, :], 0), axis=-1).reshape(slots)
    slot_lens = jnp.maximum(slot_lens, 1)

    query_own, outgoing = prepare_queries(ref_pair, queries, query_gain)
    asked = lax.all_to_all(outgoing, "pair", split_axis=0, concat_axis=0, tiled=True)
    answer_keys, answer_values, prompt_keys, prompt_values = encode(
        w_key,
        w_value,
        answer_states.reshape(ans_dev * ans_len, width),
        prompt_states.reshape(pairs_dev * prompt_len, width),
        key_gain,
    )
    mixed = owner_attention(
        slot_local,
        slot_lens,
        asked,
        answer_keys.reshape(ans_dev, ans_len, kv_width),
        answer_values.reshape(ans_dev, ans_len, kv_width),
        head_dim,
    )
    mixed_in = lax.all_to_all(mixed, "pair", split_axis=0, concat_axis=0, tiled=True)
    own_numer, own_total = prompt_attention(query_own, prompt_keys, prompt_values, prompt_len, head_dim)
    out = combine(fetch_index, own_numer, own_total, mixed_in, prompt_len, head_dim)
    return out.reshape(queries.shape)


def solution(mesh):
    in_specs = (
        P(("groups", "pair"), None, None),
        P(("groups", "pair"), None, None),
        P(("groups", "pair"), None, None),
        P("pair", None),
        P("pair", None),
        P(),
        P(),
        P("groups", None),
        P("groups"),
        P("groups"),
    )
    out_specs = P(("groups", "pair"), None, None)
    return jax.shard_map(
        per_device, mesh=mesh, in_specs=in_specs, out_specs=out_specs, check_vma=False
    )
```

```python
import functools
import jax
import jax.numpy as jnp
from jax import lax
from jax.experimental import pallas as pl
from jax.experimental.pallas import tpu as pltpu
from jax.sharding import PartitionSpec as P

norm_eps = 1e-06
VMEM = pltpu.VMEM
LIMIT = 60 * 1024 * 1024


def table_lookup(table, indices):
    match = indices[..., None] == jnp.arange(table.shape[0], dtype=jnp.int32)
    return jnp.sum(jnp.where(match, table, 0), axis=-1)


def earlier_same(owners):
    width_refs = owners.shape[-1]
    earlier = jnp.arange(width_refs)[:, None] > jnp.arange(width_refs)[None, :]
    same = owners[..., :, None] == owners[..., None, :]
    return jnp.sum(same & earlier, axis=-1)


def norm_rows(x, gain):
    scale = lax.rsqrt(jnp.mean(x * x, axis=-1, keepdims=True) + norm_eps)
    return x * scale * gain


def query_kernel(pairs, plen, heads, hd, slots, idx_ref, q_ref, gain_ref, own_ref, out_ref):
    gain = gain_ref[...]
    for two in range(heads // 2):
        parts = [
            norm_rows(q_ref[:, (2 * two + e) * hd : (2 * two + e + 1) * hd].astype(jnp.float32), gain)
            for e in range(2)
        ]
        for p in range(pairs):
            rows = jnp.concatenate([x[p * plen : (p + 1) * plen] for x in parts], axis=0)
            own_ref[p, two * 2 * plen : (two + 1) * 2 * plen, :] = rows.astype(jnp.bfloat16)

    def body(s, carry):
        out_ref[s] = own_ref[idx_ref[s]]
        return carry

    lax.fori_loop(0, slots, body, 0)


def prepare_queries(idx, queries, gain):
    pairs, plen, width = queries.shape
    hd = gain.shape[0]
    heads = width // hd
    slots = idx.shape[0]
    return pl.pallas_call(
        functools.partial(query_kernel, pairs, plen, heads, hd, slots),
        out_shape=[
            jax.ShapeDtypeStruct((pairs, heads * plen, hd), jnp.bfloat16),
            jax.ShapeDtypeStruct((slots, heads * plen, hd), jnp.bfloat16),
        ],
        in_specs=[
            pl.BlockSpec(memory_space=pltpu.SMEM),
            pl.BlockSpec(memory_space=VMEM),
            pl.BlockSpec(memory_space=VMEM),
        ],
        out_specs=[pl.BlockSpec(memory_space=VMEM)] * 2,
        compiler_params=pltpu.CompilerParams(vmem_limit_bytes=LIMIT),
    )(idx, queries.reshape(pairs * plen, width), gain.reshape(1, hd))


def project_kernel(hd, x_ref, wk_ref, wv_ref, gain_ref, k_ref, v_ref):
    x = x_ref[...]
    raw = jnp.dot(x, wk_ref[...], preferred_element_type=jnp.float32)
    for h in range(raw.shape[1] // hd):
        cols = slice(h * hd, (h + 1) * hd)
        k_ref[:, cols] = norm_rows(raw[:, cols], gain_ref[...]).astype(jnp.bfloat16)
    v_ref[...] = jnp.dot(x, wv_ref[...], preferred_element_type=jnp.float32).astype(jnp.bfloat16)


def project(x, wk, wv, gain):
    rows, width = x.shape
    kvw = wk.shape[1]
    hd = gain.shape[0]
    block = 128
    whole = pl.BlockSpec((width, kvw), lambda i: (0, 0), pipeline_mode=pl.Buffered(1))
    return pl.pallas_call(
        functools.partial(project_kernel, hd),
        grid=(rows // block,),
        out_shape=[jax.ShapeDtypeStruct((rows, kvw), jnp.bfloat16)] * 2,
        in_specs=[
            pl.BlockSpec((block, width), lambda i: (i, 0)),
            whole,
            whole,
            pl.BlockSpec((1, hd), lambda i: (0, 0)),
        ],
        out_specs=[pl.BlockSpec((block, kvw), lambda i: (i, 0))] * 2,
        compiler_params=pltpu.CompilerParams(vmem_limit_bytes=LIMIT),
    )(x, wk, wv, gain.reshape(1, hd))


def owner_kernel(per, kvh, hd, scale, slot_ref, len_ref, q_ref, k_ref, v_ref, o_ref):
    step = pl.program_id(0)
    rows = q_ref.shape[1]
    each = rows // kvh
    alen = k_ref.shape[1]
    spots = [(slice(h * each, (h + 1) * each), slice(h * hd, (h + 1) * hd)) for h in range(kvh)]
    for e in range(per):
        ref = step * per + e
        row = slot_ref[ref]
        count = len_ref[ref]
        scores = jnp.concatenate(
            [
                lax.dot_general(
                    q_ref[e, at, :], k_ref[row, :, cols], (((1,), (1,)), ((), ())),
                    preferred_element_type=jnp.float32,
                )
                for at, cols in spots
            ],
            axis=0,
        )
        position = lax.broadcasted_iota(jnp.int32, (rows, alen), 1)
        weights = jnp.where(position < count, jnp.exp(scores * scale), 0.0)
        total = jnp.sum(weights, axis=-1, keepdims=True)
        rounded = weights.astype(jnp.bfloat16)
        numer = jnp.concatenate(
            [
                jnp.dot(rounded[at], v_ref[row, :, cols], preferred_element_type=jnp.float32)
                for at, cols in spots
            ],
            axis=0,
        )
        o_ref[e, :rows, :] = (numer / total).astype(jnp.bfloat16)
        o_ref[e, rows:, :] = pack_totals(jnp.broadcast_to(total, (rows, hd)))


def pack_totals(total):
    rows, hd = total.shape
    flat = total.T[:16]
    left = [flat[:, i * hd : (i + 1) * hd] for i in range(rows // hd)]
    place = lax.broadcasted_iota(jnp.int32, (16, hd), 0)
    packed = jnp.zeros((16, hd), jnp.float32)
    at = 0
    for _ in range(3):
        for i in range(len(left)):
            term = left[i].astype(jnp.bfloat16).astype(jnp.float32)
            packed = jnp.where(place == at, term, packed)
            left[i] = left[i] - term
            at += 1
    return packed.astype(jnp.bfloat16)


def unpack_totals(packed, rows):
    hd = packed.shape[1]
    terms = packed.astype(jnp.float32)
    count = rows // hd
    flat = [
        terms[i : i + 1] + terms[count + i : count + i + 1] + terms[2 * count + i : 2 * count + i + 1]
        for i in range(count)
    ]
    return jnp.concatenate([jnp.broadcast_to(f, (hd, hd)).T for f in flat], axis=0)


def owner_attention(slot, lens, q, keys, values, hd):
    slots, rows, _ = q.shape
    _, alen, kvw = keys.shape
    per = 4
    spec = lambda shape, f: pl.BlockSpec(shape, f)
    return pl.pallas_call(
        functools.partial(owner_kernel, per, kvw // hd, hd, hd ** (-0.5)),
        grid_spec=pltpu.PrefetchScalarGridSpec(
            num_scalar_prefetch=2,
            grid=(slots // per,),
            in_specs=[
                spec((per, rows, hd), lambda i, *_: (i, 0, 0)),
                spec(keys.shape, lambda i, *_: (0, 0, 0)),
                spec(keys.shape, lambda i, *_: (0, 0, 0)),
            ],
            out_specs=spec((per, rows + 16, hd), lambda i, *_: (i, 0, 0)),
        ),
        out_shape=jax.ShapeDtypeStruct((slots, rows + 16, hd), jnp.bfloat16),
        compiler_params=pltpu.CompilerParams(vmem_limit_bytes=LIMIT),
    )(slot, lens, q, keys, values)


def prompt_kernel(per, plen, kvh, hd, scale, q_ref, k_ref, v_ref, n_ref, t_ref):
    step = pl.program_id(0)
    rows = q_ref.shape[1]
    each = rows // kvh
    keys_count = k_ref.shape[0]
    spots = [(slice(h * each, (h + 1) * each), slice(h * hd, (h + 1) * hd)) for h in range(kvh)]
    for e in range(per):
        pair = step * per + e
        place = lax.broadcasted_iota(jnp.int32, (rows, keys_count), 1)
        token = lax.broadcasted_iota(jnp.int32, (rows, keys_count), 0) % plen
        valid = (place >= pair * plen) & (place <= pair * plen + token)
        scores = jnp.concatenate(
            [
                lax.dot_general(
                    q_ref[e, at, :], k_ref[:, cols], (((1,), (1,)), ((), ())),
                    preferred_element_type=jnp.float32,
                )
                for at, cols in spots
            ],
            axis=0,
        )
        weights = jnp.where(valid, jnp.exp(scores * scale), 0.0)
        total = jnp.sum(weights, axis=-1, keepdims=True)
        rounded = weights.astype(jnp.bfloat16)
        numer = jnp.concatenate(
            [jnp.dot(rounded[at], v_ref[:, cols], preferred_element_type=jnp.float32) for at, cols in spots],
            axis=0,
        )
        mixed = (numer / total).astype(jnp.bfloat16).astype(jnp.float32)
        n_ref[e] = total * mixed
        t_ref[e] = jnp.broadcast_to(total, (rows, hd))


def prompt_attention(q, keys, values, plen, hd):
    pairs, rows, _ = q.shape
    kvw = keys.shape[1]
    per = 4
    block = pl.BlockSpec((per, rows, hd), lambda i: (i, 0, 0))
    full = pl.BlockSpec(keys.shape, lambda i: (0, 0))
    return pl.pallas_call(
        functools.partial(prompt_kernel, per, plen, kvw // hd, hd, hd ** (-0.5)),
        grid=(pairs // per,),
        in_specs=[block, full, full],
        out_specs=[block] * 2,
        out_shape=[jax.ShapeDtypeStruct((pairs, rows, hd), jnp.float32)] * 2,
        compiler_params=pltpu.CompilerParams(vmem_limit_bytes=LIMIT),
    )(q, keys, values)


def combine_kernel(per, plen, hd, at_ref, n_ref, t_ref, in_ref, o_ref):
    step = pl.program_id(0)
    rows = n_ref.shape[1]
    results = []
    for e in range(per):
        numer = n_ref[e]
        denom = t_ref[e]
        for side in range(2):
            at = at_ref[(step * per + e) * 2 + side]
            total = unpack_totals(in_ref[at, rows:, :], rows)
            numer = numer + total * in_ref[at, :rows, :].astype(jnp.float32)
            denom = denom + total
        results.append(numer / denom)
    for head in range(rows // plen):
        block = jnp.concatenate([r[head * plen : (head + 1) * plen] for r in results], axis=0)
        o_ref[:, head * hd : (head + 1) * hd] = block.astype(jnp.bfloat16)


def combine(at, numer, denom, incoming, plen, hd):
    pairs, rows, _ = numer.shape
    per = 4
    heads = rows // plen
    block = pl.BlockSpec((per, rows, hd), lambda i, *_: (i, 0, 0))
    return pl.pallas_call(
        functools.partial(combine_kernel, per, plen, hd),
        grid_spec=pltpu.PrefetchScalarGridSpec(
            num_scalar_prefetch=1,
            grid=(pairs // per,),
            in_specs=[block, block, pl.BlockSpec(incoming.shape, lambda i, *_: (0, 0, 0))],
            out_specs=pl.BlockSpec((per * plen, heads * hd), lambda i, *_: (i, 0)),
        ),
        out_shape=jax.ShapeDtypeStruct((pairs * plen, heads * hd), jnp.bfloat16),
        compiler_params=pltpu.CompilerParams(vmem_limit_bytes=LIMIT),
    )(at, numer, denom, incoming)


def ring_kernel(
    chips, seg, hd, wk_ref, wv_ref, xa_ref, xp_ref, gain_ref, ak_ref, av_ref, pk_ref, pv_ref,
    keys_buf, values_buf, x_buf, key_acc, value_acc, own_sem, x_sem,
    ring_send, ring_recv, side_send, side_recv, swap_send, swap_recv, late_send, late_recv,
):
    me = lax.axis_index("pair")
    group = lax.axis_index("groups")
    depth = wk_ref.shape[0]
    chip, core = me // 2, me % 2
    even = chip % 2
    odd_group = group % 2
    position = (1 - even) * (chip // 2) + even * (chips - 1 - chip // 2)

    def chip_at(place):
        place = (place + 2 * chips) % chips
        back = place // (chips // 2)
        return (1 - back) * 2 * place + back * (2 * (chips - 1 - place) + 1)

    right = (group, chip_at(position + 1) * 2 + core)
    left = (group, chip_at(position - 1) * 2 + core)
    sibling = (group, chip * 2 + 1 - core)
    twin = (group + 1 - 2 * odd_group, me)
    partners = (right, left)
    mesh_id = pl.DeviceIdType.MESH

    barrier = pltpu.get_barrier_semaphore()
    for other in (right, left, sibling, twin):
        pl.semaphore_signal(barrier, inc=1, device_id=other, device_id_type=mesh_id)
    own = []
    outs = (keys_buf, values_buf)
    accs = (key_acc, value_acc)
    for w, (src, out) in enumerate(((wk_ref, keys_buf), (wv_ref, values_buf))):
        place = pl.ds(pl.multiple_of(core * depth, 16), depth)
        copy = pltpu.make_async_copy(src, out.at[chip, place], own_sem.at[w])
        copy.start()
        own.append(copy)
    answers = xa_ref.shape[0]
    total_rows = x_buf.shape[0]
    x_copies = (
        pltpu.make_async_copy(xa_ref, x_buf.at[:answers], x_sem.at[0]),
        pltpu.make_async_copy(xp_ref, x_buf.at[answers:], x_sem.at[1]),
    )
    for copy in x_copies:
        copy.start()
    for copy in own:
        copy.wait()
    pl.semaphore_wait(barrier, 4)

    first = ((depth - seg) // 16 + 1) // 2 * 16
    pieces = ((odd_group * seg, first), (odd_group * seg + first, depth - seg - first))
    mine = (odd_group * (depth - seg), seg)
    other_rows = ((1 - odd_group) * (depth - seg), seg)

    def block_of(w, step, on, rows):
        at = chip_at(position - step if w == 0 else position + step)
        start, size = rows
        return outs[w].at[at, pl.ds(pl.multiple_of(on * depth + start, 16), size)]

    def remote(block, send, recv, target):
        return pltpu.make_async_remote_copy(
            src_ref=block, dst_ref=block, send_sem=send, recv_sem=recv, device_id=target, device_id_type=mesh_id
        )

    def ring(w, step, c, arriving=0):
        block = block_of(w, step + arriving, core, pieces[c])
        at = 2 * step + c
        return remote(block, ring_send.at[w, at], ring_recv.at[w, at], partners[w])

    def side(w, step, c, on):
        block = block_of(w, step, on, pieces[c])
        at = 2 * step + c
        return remote(block, side_send.at[w, at], side_recv.at[w, at], sibling)

    def swap(w, step, rows):
        block = block_of(w, step, core, rows)
        return remote(block, swap_send.at[w, step], swap_recv.at[w, step], twin)

    def late(w, step, on):
        block = block_of(w, step, on, other_rows)
        return remote(block, late_send.at[w, step], late_recv.at[w, step], sibling)

    both = [(c, w) for c in range(2) for w in range(2)]
    for c, w in both:
        ring(w, 0, c).start()
    for c, w in both:
        side(w, 0, c, core).start()
    for w in range(2):
        late(w, 0, core).start()

    def hand_over(step):
        for w in range(2):
            swap(w, step, other_rows).wait_recv()
            late(w, step, core).start()

    lag = 2
    for copy in x_copies:
        copy.wait()
    for acc in accs:
        acc[...] = jnp.zeros_like(acc)
    half = total_rows // 2

    def multiply(step):
        for w in range(2):
            for c in range(2):
                side(w, step, c, 1 - core).wait_recv()
            late(w, step, 1 - core).wait_recv()
            at = chip_at(position - step if w == 0 else position + step)
            cols = pl.ds(pl.multiple_of(at * 2 * depth, 128), 2 * depth)

            def part(i, carry):
                rows = pl.ds(pl.multiple_of(i * half, 16), half)
                accs[w][rows, :] += jnp.dot(
                    x_buf[rows, cols], outs[w][at], preferred_element_type=jnp.float32
                )
                return carry

            lax.fori_loop(0, 2, part, 0)

    def body(step, carry):
        for c, w in both:
            ring(w, step - 1, c, 1).wait_recv()

            @pl.when(step < chips - 1)
            def _():
                ring(w, step, c).start()

            side(w, step, c, core).start()
        for w in range(2):
            swap(w, step, mine).start()

        @pl.when(step > lag)
        def _():
            hand_over(step - lag)

        @pl.when(step > lag)
        def _():
            multiply(step - lag - 1)

        return carry

    lax.fori_loop(1, chips, body, 0)

    def finish(step, carry):
        hand_over(step)
        return carry

    lax.fori_loop(chips - lag, chips, finish, 0)

    def rest(step, carry):
        multiply(step)
        return carry

    lax.fori_loop(chips - lag - 1, chips, rest, 0)

    block = 128
    for i in range(total_rows // block):
        rows = slice(i * block, (i + 1) * block)
        inside = i * block < answers
        to_k, to_v = (ak_ref, av_ref) if inside else (pk_ref, pv_ref)
        to = slice(i * block - (0 if inside else answers), (i + 1) * block - (0 if inside else answers))
        for h in range(key_acc.shape[1] // hd):
            cols = slice(h * hd, (h + 1) * hd)
            to_k[to, cols] = norm_rows(key_acc[rows, cols], gain_ref[...]).astype(jnp.bfloat16)
        to_v[to, :] = value_acc[rows, :].astype(jnp.bfloat16)

    def drain(step, carry):
        for c, w in both:
            side(w, step, c, core).wait_send()

            @pl.when(step < chips - 1)
            def _():
                ring(w, step, c).wait_send()

        for w in range(2):
            late(w, step, core).wait_send()

            @pl.when(step > 0)
            def _():
                swap(w, step, mine).wait_send()

        return carry

    lax.fori_loop(0, chips, drain, 0)


def encode(w_key, w_value, answer_x, prompt_x, gain):
    peers = lax.axis_size("pair")
    depth, kvw = w_key.shape
    hd = gain.shape[0]
    if 2 * depth % 128:
        key_full, value_full = (lax.all_gather(w, "pair", axis=0, tiled=True) for w in (w_key, w_value))
        return (
            *project(answer_x, key_full, value_full, gain),
            *project(prompt_x, key_full, value_full, gain),
        )
    chips = peers // 2
    seg = max(1, round(depth // 16 * 0.45)) * 16
    answers, width = answer_x.shape
    prompts = prompt_x.shape[0]
    anywhere = pl.BlockSpec(memory_space=pl.ANY)
    vmem = pl.BlockSpec(memory_space=VMEM)
    dma = pltpu.SemaphoreType.DMA
    return pl.pallas_call(
        functools.partial(ring_kernel, chips, seg, hd),
        out_shape=[jax.ShapeDtypeStruct((n, kvw), jnp.bfloat16) for n in (answers, answers, prompts, prompts)],
        in_specs=[anywhere] * 4 + [vmem],
        out_specs=[vmem] * 4,
        scratch_shapes=[VMEM((chips, 2 * depth, kvw), jnp.bfloat16)] * 2
        + [VMEM((answers + prompts, width), jnp.bfloat16)]
        + [VMEM((answers + prompts, kvw), jnp.float32)] * 2
        + [dma((2,))] * 2
        + [dma((2, 2 * chips))] * 8,
        compiler_params=pltpu.CompilerParams(
            collective_id=0, has_side_effects=True, vmem_limit_bytes=LIMIT
        ),
    )(w_key, w_value, answer_x, prompt_x, gain.reshape(1, hd))


def per_device(
    answer_states, prompt_states, queries, w_key, w_value, key_gain, query_gain, pair_list, answer_row, lengths
):
    device = lax.axis_index("pair")
    peers = lax.axis_size("pair")
    ans_dev, ans_len, width = answer_states.shape
    pairs_dev, prompt_len = (queries.shape[0], queries.shape[1])
    head_dim = key_gain.shape[0]
    kv_width = w_key.shape[1]
    refs = 2 * pairs_dev
    capacity = (refs + peers - 1) // peers
    slots = peers * capacity

    all_ids = pair_list.reshape(peers, refs)
    all_rows = table_lookup(answer_row, all_ids)
    all_owner = all_rows // ans_dev
    all_local = all_rows % ans_dev
    all_rank = earlier_same(all_owner)
    all_lens = table_lookup(lengths, all_ids)
    my_owner = lax.dynamic_index_in_dim(all_owner, device, 0, keepdims=False)
    my_rank = lax.dynamic_index_in_dim(all_rank, device, 0, keepdims=False)
    fetch_index = my_owner * capacity + my_rank
    slot_ids = jnp.arange(slots, dtype=jnp.int32)
    ref_match = fetch_index[None, :] == slot_ids[:, None]
    ref_pair = jnp.sum(jnp.where(ref_match, jnp.arange(refs, dtype=jnp.int32)[None, :] // 2, 0), axis=1)
    slot_range = jnp.arange(capacity, dtype=jnp.int32)
    slot_match = (all_owner == device)[:, None, :] & (all_rank[:, None, :] == slot_range[None, :, None])
    slot_local = jnp.sum(jnp.where(slot_match, all_local[:, None, :], 0), axis=-1).reshape(slots)
    slot_lens = jnp.sum(jnp.where(slot_match, all_lens[:, None, :], 0), axis=-1).reshape(slots)
    slot_lens = jnp.maximum(slot_lens, 1)

    query_own, outgoing = prepare_queries(ref_pair, queries, query_gain)
    asked = lax.all_to_all(outgoing, "pair", split_axis=0, concat_axis=0, tiled=True)
    answer_keys, answer_values, prompt_keys, prompt_values = encode(
        w_key,
        w_value,
        answer_states.reshape(ans_dev * ans_len, width),
        prompt_states.reshape(pairs_dev * prompt_len, width),
        key_gain,
    )
    mixed = owner_attention(
        slot_local,
        slot_lens,
        asked,
        answer_keys.reshape(ans_dev, ans_len, kv_width),
        answer_values.reshape(ans_dev, ans_len, kv_width),
        head_dim,
    )
    mixed_in = lax.all_to_all(mixed, "pair", split_axis=0, concat_axis=0, tiled=True)
    own_numer, own_total = prompt_attention(query_own, prompt_keys, prompt_values, prompt_len, head_dim)
    out = combine(fetch_index, own_numer, own_total, mixed_in, prompt_len, head_dim)
    return out.reshape(queries.shape)


def solution(mesh):
    in_specs = (
        P(("groups", "pair"), None, None),
        P(("groups", "pair"), None, None),
        P(("groups", "pair"), None, None),
        P("pair", None),
        P("pair", None),
        P(),
        P(),
        P("groups", None),
        P("groups"),
        P("groups"),
    )
    out_specs = P(("groups", "pair"), None, None)
    return jax.shard_map(
        per_device, mesh=mesh, in_specs=in_specs, out_specs=out_specs, check_vma=False
    )
```
